128 devices in a mesh: sub: 16 (over y, x), tm: 8 (over z, core).
Axes of the slice: x: 4, y: 4, z: 4, core: 2. Of those that a mesh axis runs over, the one named last changes fastest.
Arguments:
- voltages: bfloat16 [8192, 24, 2, 2048], P('sub', 'tm'), may hold values from -6 to 6
- slot_feed: int32 [2048], replicated, may hold values from 0 to 2047, each once
- chan_lag: int32 [8192], replicated, may hold values from 0 to 4096
- trial_dm: int32 [512], replicated, may hold values from 0 to 4096
- beam_order: int32 [1024], replicated, may hold values from 0 to 1023, each once
Outputs:
- dedispersed: float32 [1024, 24, 512], P('sub', 'tm')
The draws below stay inside these ranges and needn't reach their ends.
Inputs may be any that keep to these rules, and one draw needn't show every extreme that they name: `slot_feed`: each feed once; slot (p * 4 + y) * 256 + n is polarization p at east-west position y and north-south position n. `beam_order`: each beam once.
All inputs are finite; a program needn't handle non-finite values.
Results may differ from the reference program's by a relative error of at most 0.00088.
Values may be sent and summed in bfloat16 or wider, within the bound.
A program may use at most 192 MiB of HBM per device.

```python
import math
import jax
import jax.numpy as jnp
from jax import lax

NS = 256
CYL = 4
POL = 2
CHANNELS = 8192
NDM = 512
MAXD = 6
LAG_TOP = 4096
FEEDS = 2048
BEAMS = 1024
TIME = 24
QUANT = 2796202


def shuffled_ramp(key, length):
    increments = jax.random.randint(jax.random.fold_in(key, 3), (length,), 1, 4).astype(jnp.int32)
    running = jnp.cumsum(increments).astype(jnp.int32)
    lowest = running[0]
    highest = running[length - 1]
    ramp = ((running - lowest) * LAG_TOP // (highest - lowest)).astype(jnp.int32)
    return jax.random.permutation(jax.random.fold_in(key, 5), ramp).astype(jnp.int32)


def draw_chan_lag(key, part):
    return shuffled_ramp(jax.random.fold_in(key, 11), CHANNELS)


def draw_trial_dm(key, part):
    return shuffled_ramp(jax.random.fold_in(key, 23), NDM)


def levels(stream_key, dims, pieces, smallest, high):
    factor_of = 1.0
    for axis_at, shards_of in pieces:
        steps = jax.random.uniform(jax.random.fold_in(jax.random.fold_in(stream_key, 6), axis_at), (shards_of,), jnp.float32, smallest / len(pieces), high / len(pieces))
        factor_of = factor_of * jnp.repeat(jnp.exp(steps), dims[axis_at] // shards_of).reshape((-1,) + (1,) * (len(dims) - 1 - axis_at))
    return factor_of


def gaussian(rng, dims, deviation, most, pieces=(), kind=jnp.bfloat16):
    level = levels(rng, dims, pieces, -0.22, 0.18) if pieces else 1.0
    array = jax.random.normal(rng, dims, jnp.float32) * deviation * level
    return jnp.minimum(jnp.maximum(array, -most), most).astype(kind)


def setup_inputs(seed: int = 0) -> dict:
    splits = jax.random.split(jax.random.key(seed), 6)
    return {
        "voltages": gaussian(splits[0], (CHANNELS, TIME, 2, FEEDS), 1.0, 6.0, ((0, 16), (1, 8))),
        "slot_feed": jax.random.permutation(splits[1], FEEDS).astype(jnp.int32),
        "chan_lag": draw_chan_lag(jax.random.fold_in(splits[5], 71), 0),
        "trial_dm": draw_trial_dm(jax.random.fold_in(splits[5], 71), 0),
        "beam_order": jax.random.permutation(splits[4], BEAMS).astype(jnp.int32),
    }


def north_table():
    positions = jnp.arange(NS, dtype=jnp.int32)
    phase_index = positions[:, None] * positions[None, :] % NS
    angles = phase_index.astype(jnp.float32) * (2.0 * math.pi / NS)
    cosine = jnp.cos(angles) / math.sqrt(NS)
    sine_part = jnp.sin(angles) / math.sqrt(NS)
    real_row = jnp.stack([cosine, -sine_part], axis=1)
    imag_row = jnp.stack([sine_part, cosine], axis=1)
    return jnp.stack([real_row, imag_row], axis=0).astype(jnp.bfloat16)

def west_table():
    cylinder = jnp.arange(CYL, dtype=jnp.int32)
    quarter_turn = cylinder[:, None] * cylinder[None, :] % 4
    cosine = (quarter_turn == 0).astype(jnp.float32) - (quarter_turn == 2).astype(jnp.float32)
    sine_part = (quarter_turn == 1).astype(jnp.float32) - (quarter_turn == 3).astype(jnp.float32)
    real_row = jnp.stack([cosine, -sine_part], axis=2)
    imag_row = jnp.stack([sine_part, cosine], axis=2)
    return 0.5 * jnp.stack([real_row, imag_row], axis=1)

def compute_power(north_beams):
    west_beams = jnp.einsum('ctpyom,yoeq->ctpeqm', north_beams, west_table(), precision=lax.Precision.HIGHEST)
    squares = lax.optimization_barrier(jnp.sum(west_beams * west_beams, axis=(2, 4)))
    return squares.reshape(north_beams.shape[0], north_beams.shape[1], CYL * NS)

def delay_table(lag_rows, trial_dm):
    return (lag_rows[:, None] * trial_dm[None, :] // QUANT).astype(jnp.int32)

def reference(voltages, slot_feed, chan_lag, trial_dm, beam_order):
    width = 64
    blocks = CHANNELS // width
    samples = voltages.shape[1]
    table = north_table().astype(jnp.float32)

    def accumulate(accumulated, inputs):
        volt_block, lag_rows = inputs
        grid_volts = jnp.take(volt_block, slot_feed, axis=3).reshape(width, samples, 2, POL, CYL, NS)
        north_beams = jnp.einsum('ctrpyn,rnom->ctpyom', grid_volts.astype(jnp.float32), table, precision=lax.Precision.HIGHEST)
        intensity = compute_power(north_beams)
        ordered = jnp.take(intensity, beam_order, axis=2)
        average = lax.optimization_barrier(jnp.sum(ordered, axis=1)) / samples
        normal = (ordered - average[:, None, :]).astype(jnp.bfloat16)
        source = normal.astype(jnp.float32)
        delays = delay_table(lag_rows, trial_dm)
        for delay_step in range(MAXD + 1):
            onehot = (delays == delay_step).astype(jnp.float32)
            part = jnp.einsum('ctb,cd->btd', source, onehot, precision=lax.Precision.HIGHEST)
            moved = jnp.pad(part, ((0, 0), (delay_step, 0), (0, 0)))[:, :samples, :]
            accumulated = accumulated + moved
        return (accumulated, None)
    initial = jnp.zeros((BEAMS, samples, NDM), jnp.float32)
    accumulated, ignored = lax.scan(accumulate, initial, (voltages.reshape(blocks, width, samples, 2, FEEDS), chan_lag.reshape(blocks, width)))
    return accumulated / math.sqrt(CHANNELS)
```

```python
import functools
import math

import jax
import jax.numpy as jnp
from jax import lax
from jax.experimental import pallas as pl
from jax.experimental.pallas import tpu as pltpu
from jax.sharding import PartitionSpec as P

NS = 256
CYL = 4
POL = 2
CHANNELS = 8192
NDM = 512
MAXD = 6
QUANT = 2796202
FEEDS = 2048
BEAMS = 1024
TIME = 24
CHUNKS = 2
AXES = ("sub", "tm")


def north_table():
    positions = jnp.arange(NS, dtype=jnp.int32)
    phase_index = positions[:, None] * positions[None, :] % NS
    angles = phase_index.astype(jnp.float32) * (2.0 * math.pi / NS)
    cosine = jnp.cos(angles) / math.sqrt(NS)
    sine_part = jnp.sin(angles) / math.sqrt(NS)
    real_row = jnp.stack([cosine, -sine_part], axis=1)
    imag_row = jnp.stack([sine_part, cosine], axis=1)
    table = jnp.stack([real_row, imag_row], axis=0).astype(jnp.bfloat16)
    return table.reshape(2 * NS, 2 * NS)


def form_kernel(volt_ref, feed_ref, table_ref, order_ref, out_ref, grid_ref):
    chans = volt_ref.shape[0]
    rows = volt_ref[:, 0].reshape(2 * chans, FEEDS)
    half = NS // 2

    def slots(at, phase):
        tiles = [grid_ref[at // half + i, pl.ds(phase, chans, stride=2), :] for i in range(2)]
        return jnp.concatenate(tiles, axis=1).astype(jnp.bfloat16)

    placed = jnp.dot(rows, feed_ref[...], preferred_element_type=jnp.float32)
    for tile in range(FEEDS // half):
        grid_ref[tile] = placed[:, tile * half : (tile + 1) * half]
    power = [None] * CYL
    for p in range(POL):
        re, im = [], []
        for y in range(CYL):
            at = (p * CYL + y) * NS
            pair = jnp.concatenate([slots(at, 0), slots(at, 1)], axis=1)
            north = jnp.dot(pair, table_ref[...], preferred_element_type=jnp.float32)
            re.append(north[:, :NS])
            im.append(north[:, NS:])
        a_re, a_im = re[0] + re[2], im[0] + im[2]
        b_re, b_im = re[0] - re[2], im[0] - im[2]
        c_re, c_im = re[1] + re[3], im[1] + im[3]
        d_re, d_im = re[1] - re[3], im[1] - im[3]
        west = [
            (a_re + c_re, a_im + c_im),
            (b_re + d_im, b_im - d_re),
            (a_re - c_re, a_im - c_im),
            (b_re - d_im, b_im + d_re),
        ]
        for e, (w_re, w_im) in enumerate(west):
            square = w_re * w_re + w_im * w_im
            power[e] = square if power[e] is None else power[e] + square
    intensity = 0.25 * jnp.concatenate(power, axis=1)
    high = intensity.astype(jnp.bfloat16)
    rest = intensity - high.astype(jnp.float32)
    mid = rest.astype(jnp.bfloat16)
    low = (rest - mid.astype(jnp.float32)).astype(jnp.bfloat16)
    total = None
    for piece in (high, mid, low):
        part = lax.dot_general(
            order_ref[...], piece, (((1,), (1,)), ((), ())), preferred_element_type=jnp.float32
        )
        total = part if total is None else total + part
    out_ref[...] = total.reshape(out_ref.shape)


def form_beams(voltages, feed_onehot, table, order_onehot, chunk, chans):
    samples = voltages.shape[1]
    block = 256
    steps = chans // block
    first = chunk * steps
    groups = BEAMS // 8
    whole = pl.BlockSpec(memory_space=pltpu.VMEM)
    return pl.pallas_call(
        form_kernel,
        grid=(steps, samples),
        in_specs=[
            pl.BlockSpec((block, 1, 2, FEEDS), lambda c, t: (first + c, t, 0, 0)),
            whole,
            whole,
            whole,
        ],
        out_specs=pl.BlockSpec((groups, 1, 8, block), lambda c, t: (0, t, 0, c)),
        out_shape=jax.ShapeDtypeStruct((groups, samples, 8, chans), jnp.float32),
        scratch_shapes=[pltpu.VMEM((FEEDS // 128, 2 * block, 128), jnp.float32)],
        compiler_params=pltpu.CompilerParams(vmem_limit_bytes=56 * 2**20),
        cost_estimate=pl.CostEstimate(
            flops=int(2 * chans * samples * (2 * FEEDS * FEEDS + 8 * 512 * 512 + 3 * BEAMS * BEAMS)),
            bytes_accessed=chans * samples * 2 * FEEDS * 4,
            transcendentals=0,
        ),
        name="form_beams",
    )(voltages, feed_onehot, table, order_onehot)


def sum_kernel(last, held_ref, lag_ref, trial_ref, before_ref, out_ref):
    chans = held_ref.shape[-1]
    step = pl.program_id(0)

    @pl.when(step == 0)
    def _():
        out_ref[...] = before_ref[...]

    held = held_ref[...].reshape(TIME, 8, chans)
    average = jnp.sum(held, axis=0) / TIME
    normal = (held - average[None]).reshape(TIME * 8, chans).astype(jnp.bfloat16)
    lag_rows = jnp.broadcast_to(lag_ref[0], (8, chans))
    lag = jnp.transpose(lag_rows)[:, :1]
    product = lag * trial_ref[...]
    delay = jnp.floor(product * (1.0 / QUANT)).astype(jnp.bfloat16)
    for k in range(MAXD + 1):
        onehot = jnp.where(delay == k, 1.0, 0.0).astype(jnp.bfloat16)
        keep = TIME * 8 - 8 * k
        rows = -(-keep // 16) * 16
        part = jnp.dot(normal[:rows], onehot, preferred_element_type=jnp.float32)
        out_ref[8 * k :, :] += part[:keep]

    if last:

        @pl.when(step == pl.num_programs(0) - 1)
        def _():
            out_ref[...] = out_ref[...] * (1.0 / math.sqrt(CHANNELS))


def sum_delays(held, lags, trials, before, last):
    chans = held.shape[-1]
    subs = lags.shape[0]
    shards = held.shape[0] // subs
    samples = held.shape[1]
    rows = TIME * 8
    return pl.pallas_call(
        functools.partial(sum_kernel, last),
        grid=(subs,),
        in_specs=[
            pl.BlockSpec((shards, samples, 8, chans), lambda s: (s, 0, 0, 0)),
            pl.BlockSpec((1, 1, chans), lambda s: (s, 0, 0)),
            pl.BlockSpec(memory_space=pltpu.VMEM),
            pl.BlockSpec(memory_space=pltpu.VMEM),
        ],
        out_specs=pl.BlockSpec((rows, NDM), lambda s: (0, 0)),
        out_shape=jax.ShapeDtypeStruct((rows, NDM), jnp.float32),
        compiler_params=pltpu.CompilerParams(vmem_limit_bytes=48 * 2**20),
        cost_estimate=pl.CostEstimate(
            flops=2 * subs * chans * rows * NDM * 7,
            bytes_accessed=subs * chans * rows * 4,
            transcendentals=0,
        ),
        name="sum_delays",
    )(held, lags, trials, before)


def per_device(voltages, slot_feed, chan_lag, trial_dm, beam_order):
    samples = voltages.shape[1]
    subs, shards = lax.axis_size("sub"), lax.axis_size("tm")
    feeds = jnp.arange(FEEDS, dtype=jnp.int32)
    feed_onehot = (feeds[:, None] == slot_feed[None, :]).astype(jnp.bfloat16)
    beams = jnp.arange(BEAMS, dtype=jnp.int32)
    order_onehot = (beam_order[:, None] == beams[None, :]).astype(jnp.bfloat16)
    table = north_table()
    lags = chan_lag.astype(jnp.float32).reshape(subs, CHUNKS, -1)
    trials = trial_dm.astype(jnp.float32).reshape(1, NDM)
    chans = voltages.shape[0] // CHUNKS
    total = jnp.zeros((TIME * 8, NDM), jnp.float32)
    for chunk in range(CHUNKS):
        formed = form_beams(voltages, feed_onehot, table, order_onehot, chunk, chans)
        held = lax.all_to_all(formed, AXES, 0, 0)
        total = sum_delays(held, lags[:, chunk : chunk + 1], trials, total, chunk == CHUNKS - 1)
    parts = lax.all_to_all(total.reshape(shards, samples, 8, NDM), "tm", 0, 0)
    return parts.transpose(0, 2, 1, 3).reshape(shards * 8, samples, NDM)


def solution(mesh):
    placed = (P("sub", "tm", None, None), P(), P(), P(), P())
    return jax.shard_map(
        per_device, mesh=mesh, in_specs=placed, out_specs=P("sub", "tm", None), check_vma=False
    )
```

```python
import functools
import math

import jax
import jax.numpy as jnp
import ml_dtypes
import numpy as np
from jax import lax
from jax.experimental import pallas as pl
from jax.experimental.pallas import tpu as pltpu
from jax.sharding import PartitionSpec as P

NS = 256
CYL = 4
POL = 2
CHANNELS = 8192
NDM = 512
MAXD = 6
QUANT = 2796202
FEEDS = 2048
BEAMS = 1024
TIME = 24
CHUNKS = 2
LEVELS = 65535.0
HALF = 32768.0
STEPS = 256.0
GROUPS = 8
ROOM = 64
SAMPLE_ROWS = 48
ROWS = 56
AXES = ("sub", "tm")


def half_table():
    n = np.arange(NS)[:, None]
    m = np.arange(NS // 2)[None, :]
    angles = (n * m % NS) * (2.0 * math.pi / NS)
    cosine = np.cos(angles) / math.sqrt(NS)
    sine = np.sin(angles) / math.sqrt(NS)
    sine[:, 0] = np.cos((np.arange(NS) * (NS // 2) % NS) * (2.0 * math.pi / NS)) / math.sqrt(NS)
    return np.concatenate([cosine, sine], axis=1).astype(np.float32).astype(ml_dtypes.bfloat16)


def as_onehot(hit):
    return hit.astype(jnp.float32).astype(jnp.bfloat16)


def column_of(row):
    return jnp.transpose(jnp.broadcast_to(row, (8, row.shape[1])))[:, :1]


def route_kernel(feed_ref, order_ref, table_ref, first_ref, second_ref, pick_ref, deepest_ref):
    deepest = jnp.zeros((), jnp.int32)
    codes = []
    above = lax.broadcasted_iota(jnp.int32, (NS, NS), 0) < lax.broadcasted_iota(jnp.int32, (NS, NS), 1)
    for d in range(GROUPS):
        block = feed_ref[:, d * NS : (d + 1) * NS] // NS
        same = (column_of(block) == block) & above
        rank = jnp.sum(same.astype(jnp.float32), axis=0, keepdims=True).astype(jnp.int32)
        deepest = jnp.maximum(deepest, jnp.max(rank))
        odd = block % 2
        flip = odd if d % 2 == 0 else 1 - odd
        codes.append((jnp.where(odd == 0, d, d ^ 1)) * ROOM + rank)
        place = block // 2 * (2 * ROOM) + flip * ROOM + rank
        hit = lax.broadcasted_iota(jnp.int32, (GROUPS * ROOM, NS), 0) == place
        second_ref[d] = jnp.dot(
            as_onehot(hit), table_ref[...], preferred_element_type=jnp.float32
        ).astype(jnp.bfloat16)
    code = jnp.concatenate(codes, axis=1).astype(jnp.float32)
    for b in range(GROUPS):
        feeds = lax.broadcasted_iota(jnp.int32, (NS, FEEDS), 0) + b * NS
        mine = jnp.sum(jnp.where(feeds == feed_ref[...], code, 0.0), axis=1, keepdims=True)
        lanes = lax.broadcasted_iota(jnp.int32, (NS, GROUPS * ROOM), 1)
        first_ref[b] = as_onehot(mine.astype(jnp.int32) == lanes)
    north = order_ref[...] % NS
    wanted = order_ref[...] - north + jnp.where(north <= NS // 2, north, NS + NS // 2 - north)
    pick_ref[...] = as_onehot(column_of(wanted) == lax.broadcasted_iota(jnp.int32, (BEAMS, BEAMS), 1))
    deepest_ref[0] = deepest


def route(slot_feed, beam_order, table):
    whole = pl.BlockSpec(memory_space=pltpu.VMEM)
    return pl.pallas_call(
        route_kernel,
        in_specs=[whole, whole, whole],
        out_specs=[whole, whole, whole, pl.BlockSpec(memory_space=pltpu.SMEM)],
        out_shape=[
            jax.ShapeDtypeStruct((GROUPS, NS, GROUPS * ROOM), jnp.bfloat16),
            jax.ShapeDtypeStruct((GROUPS, GROUPS * ROOM, NS), jnp.bfloat16),
            jax.ShapeDtypeStruct((BEAMS, BEAMS), jnp.bfloat16),
            jax.ShapeDtypeStruct((1,), jnp.int32),
        ],
        compiler_params=pltpu.CompilerParams(vmem_limit_bytes=56 * 2**20),
        name="route",
    )(slot_feed, beam_order, table)


def form_kernel(
    volt_ref, feed_ref, table_ref, first_ref, second_ref, pick_ref, deepest_ref, out_ref, grid_ref, unit_ref
):
    chans = volt_ref.shape[0]
    half = NS // 2
    t = pl.program_id(1)

    @pl.when(t == 0)
    def _():
        unit_ref[...] = jnp.zeros_like(unit_ref)

    @pl.when(deepest_ref[0] < ROOM)
    def _():
        rows = volt_ref[:, 0].reshape(2 * chans, FEEDS)
        low_half = lax.broadcasted_iota(jnp.int32, (2 * chans, half), 1) < ROOM
        pieces = [[] for _ in range(GROUPS)]
        for q in range(GROUPS // 2):
            ways = []
            for b in (2 * q, 2 * q + 1):
                way = jnp.dot(
                    rows[:, b * NS : (b + 1) * NS], first_ref[b], preferred_element_type=jnp.float32
                )
                ways.append(way)
            for v in range(GROUPS // 2):
                one = ways[0][:, v * half : (v + 1) * half]
                two = ways[1][:, v * half : (v + 1) * half]
                pieces[2 * v].append(jnp.where(low_half, one, two).astype(jnp.bfloat16))
                pieces[2 * v + 1].append(jnp.where(low_half, two, one).astype(jnp.bfloat16))
        for d in range(GROUPS):
            wave = jnp.dot(
                jnp.concatenate(pieces[d], axis=1), second_ref[d], preferred_element_type=jnp.float32
            )
            grid_ref[2 * d] = wave[:, :half]
            grid_ref[2 * d + 1] = wave[:, half:]

    @pl.when(deepest_ref[0] >= ROOM)
    def _():
        rows = volt_ref[:, 0].reshape(2 * chans, FEEDS)
        for d in range(GROUPS):
            feeds = lax.broadcasted_iota(jnp.int32, (FEEDS, NS), 0)
            place = as_onehot(feeds == feed_ref[:, d * NS : (d + 1) * NS])
            slots = jnp.dot(rows, place, preferred_element_type=jnp.float32).astype(jnp.bfloat16)
            wave = jnp.dot(slots, table_ref[...], preferred_element_type=jnp.float32)
            grid_ref[2 * d] = wave[:, :half]
            grid_ref[2 * d + 1] = wave[:, half:]

    edge = lax.broadcasted_iota(jnp.int32, (chans, half), 1) == 0

    def west(p, part):
        re, im = [], []
        for y in range(CYL):
            tile = 2 * (p * CYL + y) + part
            re.append(grid_ref[tile, pl.ds(0, chans, stride=2), :])
            im.append(grid_ref[tile, pl.ds(1, chans, stride=2), :])
        a_re, a_im = re[0] + re[2], im[0] + im[2]
        b_re, b_im = re[0] - re[2], im[0] - im[2]
        c_re, c_im = re[1] + re[3], im[1] + im[3]
        d_re, d_im = re[1] - re[3], im[1] - im[3]
        return [
            (a_re + c_re, a_im + c_im),
            (b_re + d_im, b_im - d_re),
            (a_re - c_re, a_im - c_im),
            (b_re - d_im, b_im + d_re),
        ]

    power = [None] * (2 * CYL)
    for p in range(POL):
        for e, ((c_re, c_im), (s_re, s_im)) in enumerate(zip(west(p, 0), west(p, 1))):
            t_re, t_im = jnp.where(edge, 0.0, s_re), jnp.where(edge, 0.0, s_im)
            u_re, u_im = c_re + t_im, c_im - t_re
            v_re, v_im = jnp.where(edge, s_re, c_re - t_im), jnp.where(edge, s_im, c_im + t_re)
            for at, (w_re, w_im) in ((2 * e, (u_re, u_im)), (2 * e + 1, (v_re, v_im))):
                square = w_re * w_re + w_im * w_im
                power[at] = square if power[at] is None else power[at] + square
    power = jnp.concatenate(power, axis=1)
    most = jnp.maximum(jnp.max(power, axis=1, keepdims=True), 1e-30)
    level = jnp.ceil(jnp.log2(most) * STEPS) + 1.0
    scale = LEVELS * jnp.exp2(level * (-1.0 / STEPS))
    code = jnp.floor(power * scale + 0.5)
    high = jnp.floor(code * (1.0 / 256.0)) * 256.0
    low = (code - high).astype(jnp.bfloat16)
    total = None
    for piece in (high.astype(jnp.bfloat16), low):
        part = lax.dot_general(
            pick_ref[...], piece, (((1,), (1,)), ((), ())), preferred_element_type=jnp.float32
        )
        total = part if total is None else total + part
    total = (total - HALF).reshape(BEAMS // 8, 8, chans)
    both = jnp.concatenate([total[:, :, : chans // 2], total[:, :, chans // 2 :]], axis=1)
    out_ref[:, pl.ds(pl.multiple_of(16 * t, 16), 16), :] = both.astype(jnp.int32).astype(jnp.int16)
    levels = jnp.transpose(jnp.broadcast_to(level, (chans, 128)))[:1]
    unit_ref[pl.ds(2 * t, 1), :] = levels[:, : chans // 2]
    unit_ref[pl.ds(2 * t + 1, 1), :] = levels[:, chans // 2 :]

    @pl.when(t == pl.num_programs(1) - 1)
    def _():
        levels = jnp.concatenate([unit_ref[...], jnp.zeros_like(unit_ref)], axis=0)
        levels = levels.astype(jnp.int32).astype(jnp.int16)
        groups = out_ref.shape[0]
        out_ref[:, SAMPLE_ROWS:, :] = jnp.broadcast_to(
            levels[None, : out_ref.shape[1] - SAMPLE_ROWS], (groups, out_ref.shape[1] - SAMPLE_ROWS, chans // 2)
        )


def form_beams(voltages, slot_feed, table, first, second, pick, deepest, chunk, chans):
    samples = voltages.shape[1]
    block = 256
    steps = chans // block
    base = chunk * steps
    groups = BEAMS // 8
    whole = pl.BlockSpec(memory_space=pltpu.VMEM)
    return pl.pallas_call(
        form_kernel,
        grid=(steps, samples),
        in_specs=[
            pl.BlockSpec((block, 1, 2, FEEDS), lambda c, t: (base + c, t, 0, 0)),
            whole,
            whole,
            whole,
            whole,
            whole,
            pl.BlockSpec(memory_space=pltpu.SMEM),
        ],
        out_specs=pl.BlockSpec((groups, ROWS, block // 2), lambda c, t: (0, 0, c)),
        out_shape=jax.ShapeDtypeStruct((groups, ROWS, chans // 2), jnp.int16),
        scratch_shapes=[
            pltpu.VMEM((FEEDS // 128, 2 * block, 128), jnp.float32),
            pltpu.VMEM((8, block // 2), jnp.float32),
        ],
        compiler_params=pltpu.CompilerParams(vmem_limit_bytes=56 * 2**20),
        cost_estimate=pl.CostEstimate(
            flops=int(2 * chans * samples * (2 * FEEDS * 512 + 2 * 8 * 512 * 256 + 2 * BEAMS * BEAMS)),
            bytes_accessed=chans * samples * 2 * FEEDS * 4,
            transcendentals=0,
        ),
        name="form_beams",
    )(voltages, slot_feed, table, first, second, pick, deepest)


def sum_kernel(last, held_ref, lag_ref, trial_ref, before_ref, out_ref):
    chans = 2 * held_ref.shape[-1]
    step = pl.program_id(0)

    @pl.when(step == 0)
    def _():
        out_ref[...] = before_ref[...]

    shards = held_ref.shape[0]
    code = held_ref[:, :SAMPLE_ROWS, :].reshape(TIME, 16, chans // 2).astype(jnp.float32) + HALF
    code = jnp.concatenate([code[:, :8], code[:, 8:]], axis=2)
    level = held_ref[:, SAMPLE_ROWS:, :].astype(jnp.float32)
    unit = jnp.exp2(level[:, :8] * (1.0 / STEPS)) * (0.25 / LEVELS)
    parts = []
    for shard in range(shards):
        for t in range(TIME // shards):
            row = jnp.concatenate(
                [unit[shard, 2 * t : 2 * t + 1], unit[shard, 2 * t + 1 : 2 * t + 2]], axis=1
            )
            parts.append(code[shard * (TIME // shards) + t] * row)
    held = jnp.stack(parts)
    average = jnp.sum(held, axis=0) / TIME
    normal = (held - average[None]).reshape(TIME * 8, chans).astype(jnp.bfloat16)
    lag = jnp.transpose(jnp.broadcast_to(lag_ref[0], (8, chans)))[:, :1]
    product = lag * trial_ref[...]
    delay = jnp.floor(product * (1.0 / QUANT)).astype(jnp.bfloat16)
    one, zero = jnp.ones((), jnp.bfloat16), jnp.zeros((), jnp.bfloat16)
    for k in range(MAXD + 1):
        onehot = jnp.where(delay == jnp.bfloat16(k), one, zero)
        keep = TIME * 8 - 8 * k
        rows = -(-keep // 16) * 16
        part = jnp.dot(normal[:rows], onehot, preferred_element_type=jnp.float32)
        out_ref[8 * k :, :] += part[:keep]

    if last:

        @pl.when(step == pl.num_programs(0) - 1)
        def _():
            out_ref[...] = out_ref[...] * (1.0 / math.sqrt(CHANNELS))


def sum_delays(held, lags, trials, before, last):
    chans = 2 * held.shape[-1]
    subs = lags.shape[0]
    shards = held.shape[0] // subs
    rows = TIME * 8
    return pl.pallas_call(
        functools.partial(sum_kernel, last),
        grid=(subs,),
        in_specs=[
            pl.BlockSpec((shards, ROWS, chans // 2), lambda s: (s, 0, 0)),
            pl.BlockSpec((1, 1, chans), lambda s: (s, 0, 0)),
            pl.BlockSpec(memory_space=pltpu.VMEM),
            pl.BlockSpec(memory_space=pltpu.VMEM),
        ],
        out_specs=pl.BlockSpec((rows, NDM), lambda s: (0, 0)),
        out_shape=jax.ShapeDtypeStruct((rows, NDM), jnp.float32),
        compiler_params=pltpu.CompilerParams(vmem_limit_bytes=56 * 2**20),
        cost_estimate=pl.CostEstimate(
            flops=2 * subs * chans * rows * NDM * 7,
            bytes_accessed=subs * chans * rows * 2,
            transcendentals=0,
        ),
        name="sum_delays",
    )(held, lags, trials, before)


def per_device(voltages, slot_feed, chan_lag, trial_dm, beam_order):
    samples = voltages.shape[1]
    subs, shards = lax.axis_size("sub"), lax.axis_size("tm")
    table = jnp.asarray(half_table())
    lags = chan_lag.astype(jnp.float32).reshape(subs, CHUNKS, -1)
    trials = trial_dm.astype(jnp.float32).reshape(1, NDM)
    feeds = slot_feed.reshape(1, FEEDS)
    order = beam_order.reshape(1, BEAMS)
    chans = voltages.shape[0] // CHUNKS
    total = jnp.zeros((TIME * 8, NDM), jnp.float32)
    first, second, pick, deepest = route(feeds, order, table)
    for chunk in range(CHUNKS):
        formed = form_beams(voltages, feeds, table, first, second, pick, deepest, chunk, chans)
        held = lax.all_to_all(formed, AXES, 0, 0)
        total = sum_delays(held, lags[:, chunk : chunk + 1], trials, total, chunk == CHUNKS - 1)
    parts = lax.all_to_all(total.reshape(shards, samples, 8, NDM), "tm", 0, 0)
    return parts.transpose(0, 2, 1, 3).reshape(shards * 8, samples, NDM)


def solution(mesh):
    placed = (P("sub", "tm", None, None), P(), P(), P(), P())
    return jax.shard_map(
        per_device, mesh=mesh, in_specs=placed, out_specs=P("sub", "tm", None), check_vma=False
    )
```

```python
import functools
import math

import jax
import jax.numpy as jnp
import ml_dtypes
import numpy as np
from jax import lax
from jax.experimental import pallas as pl
from jax.experimental.pallas import tpu as pltpu
from jax.sharding import PartitionSpec as P

NS = 256
CYL = 4
POL = 2
CHANNELS = 8192
NDM = 512
MAXD = 6
QUANT = 2796202
FEEDS = 2048
BEAMS = 1024
TIME = 24
CHUNKS = 2
LEVELS = 65535.0
HALF = 32768.0
STEPS = 256.0
ROUND = 12582912.0
SLAB = 32
TOGETHER = 8
GROUPS = 8
ROOM = 64
SAMPLE_ROWS = 48
ROWS = 56
AXES = ("sub", "tm")


def half_table():
    n = np.arange(NS)[:, None]
    m = np.arange(NS // 2)[None, :]
    angles = (n * m % NS) * (2.0 * math.pi / NS)
    cosine = np.cos(angles) / math.sqrt(NS)
    sine = np.sin(angles) / math.sqrt(NS)
    sine[:, 0] = np.cos((np.arange(NS) * (NS // 2) % NS) * (2.0 * math.pi / NS)) / math.sqrt(NS)
    return np.concatenate([cosine, sine], axis=1).astype(np.float32).astype(ml_dtypes.bfloat16)


def as_onehot(hit):
    return hit.astype(jnp.float32).astype(jnp.bfloat16)


def column_of(row):
    return jnp.transpose(jnp.broadcast_to(row, (8, row.shape[1])))[:, :1]


def route_kernel(feed_ref, order_ref, table_ref, first_ref, second_ref, pick_ref, deepest_ref):
    deepest = jnp.zeros((), jnp.int32)
    codes = []
    above = lax.broadcasted_iota(jnp.int32, (NS, NS), 0) < lax.broadcasted_iota(jnp.int32, (NS, NS), 1)
    for d in range(GROUPS):
        block = feed_ref[:, d * NS : (d + 1) * NS] // NS
        same = (column_of(block) == block) & above
        rank = jnp.sum(same.astype(jnp.float32), axis=0, keepdims=True).astype(jnp.int32)
        deepest = jnp.maximum(deepest, jnp.max(rank))
        odd = block % 2
        flip = odd if d % 2 == 0 else 1 - odd
        codes.append((jnp.where(odd == 0, d, d ^ 1)) * ROOM + rank)
        place = block // 2 * (2 * ROOM) + flip * ROOM + rank
        hit = lax.broadcasted_iota(jnp.int32, (GROUPS * ROOM, NS), 0) == place
        second_ref[d] = jnp.dot(
            as_onehot(hit), table_ref[...], preferred_element_type=jnp.float32
        ).astype(jnp.bfloat16)
    code = jnp.concatenate(codes, axis=1).astype(jnp.float32)
    for b in range(GROUPS):
        feeds = lax.broadcasted_iota(jnp.int32, (NS, FEEDS), 0) + b * NS
        mine = jnp.sum(jnp.where(feeds == feed_ref[...], code, 0.0), axis=1, keepdims=True)
        lanes = lax.broadcasted_iota(jnp.int32, (NS, GROUPS * ROOM), 1)
        first_ref[b] = as_onehot(mine.astype(jnp.int32) == lanes)
    north = order_ref[...] % NS
    wanted = order_ref[...] - north + jnp.where(north <= NS // 2, north, NS + NS // 2 - north)
    pick_ref[...] = as_onehot(column_of(wanted) == lax.broadcasted_iota(jnp.int32, (BEAMS, BEAMS), 1))
    deepest_ref[0] = deepest


def route(slot_feed, beam_order, table):
    whole = pl.BlockSpec(memory_space=pltpu.VMEM)
    return pl.pallas_call(
        route_kernel,
        in_specs=[whole, whole, whole],
        out_specs=[whole, whole, whole, pl.BlockSpec(memory_space=pltpu.SMEM)],
        out_shape=[
            jax.ShapeDtypeStruct((GROUPS, NS, GROUPS * ROOM), jnp.bfloat16),
            jax.ShapeDtypeStruct((GROUPS, GROUPS * ROOM, NS), jnp.bfloat16),
            jax.ShapeDtypeStruct((BEAMS, BEAMS), jnp.bfloat16),
            jax.ShapeDtypeStruct((1,), jnp.int32),
        ],
        compiler_params=pltpu.CompilerParams(vmem_limit_bytes=56 * 2**20),
        name="route",
    )(slot_feed, beam_order, table)


def form_kernel(
    volt_ref, feed_ref, table_ref, first_ref, second_ref, pick_ref, deepest_ref, out_ref,
    grid_ref, unit_ref, power_ref, peak_ref, high_ref, low_ref,
):
    chans = volt_ref.shape[0]
    half = NS // 2
    t = pl.program_id(1)

    @pl.when(t == 0)
    def _():
        unit_ref[...] = jnp.zeros_like(unit_ref)

    @pl.when(deepest_ref[0] < ROOM)
    def _():
        rows = volt_ref[:, 0].reshape(2 * chans, FEEDS)
        low_half = lax.broadcasted_iota(jnp.int32, (2 * chans, half), 1) < ROOM
        pieces = [[] for _ in range(GROUPS)]
        for q in range(GROUPS // 2):
            ways = []
            for b in (2 * q, 2 * q + 1):
                way = jnp.dot(
                    rows[:, b * NS : (b + 1) * NS], first_ref[b], preferred_element_type=jnp.float32
                )
                ways.append(way)
            for v in range(GROUPS // 2):
                one = ways[0][:, v * half : (v + 1) * half]
                two = ways[1][:, v * half : (v + 1) * half]
                pieces[2 * v].append(jnp.where(low_half, one, two).astype(jnp.bfloat16))
                pieces[2 * v + 1].append(jnp.where(low_half, two, one).astype(jnp.bfloat16))
        for d in range(GROUPS):
            wave = jnp.dot(
                jnp.concatenate(pieces[d], axis=1), second_ref[d], preferred_element_type=jnp.float32
            )
            grid_ref[2 * d] = wave[:, :half]
            grid_ref[2 * d + 1] = wave[:, half:]

    @pl.when(deepest_ref[0] >= ROOM)
    def _():
        rows = volt_ref[:, 0].reshape(2 * chans, FEEDS)
        for d in range(GROUPS):
            feeds = lax.broadcasted_iota(jnp.int32, (FEEDS, NS), 0)
            place = as_onehot(feeds == feed_ref[:, d * NS : (d + 1) * NS])
            slots = jnp.dot(rows, place, preferred_element_type=jnp.float32).astype(jnp.bfloat16)
            wave = jnp.dot(slots, table_ref[...], preferred_element_type=jnp.float32)
            grid_ref[2 * d] = wave[:, :half]
            grid_ref[2 * d + 1] = wave[:, half:]

    edge = lax.broadcasted_iota(jnp.int32, (SLAB, half), 1) == 0

    def west(p, part, at):
        re, im = [], []
        for y in range(CYL):
            tile = 2 * (p * CYL + y) + part
            re.append(grid_ref[tile, pl.ds(2 * at, SLAB, stride=2), :])
            im.append(grid_ref[tile, pl.ds(2 * at + 1, SLAB, stride=2), :])
        a_re, a_im = re[0] + re[2], im[0] + im[2]
        b_re, b_im = re[0] - re[2], im[0] - im[2]
        c_re, c_im = re[1] + re[3], im[1] + im[3]
        d_re, d_im = re[1] - re[3], im[1] - im[3]
        return [
            (a_re + c_re, a_im + c_im),
            (b_re + d_im, b_im - d_re),
            (a_re - c_re, a_im - c_im),
            (b_re - d_im, b_im + d_re),
        ]

    for at in range(0, chans, SLAB):
        power = [None] * (2 * CYL)
        for p in range(POL):
            for e, ((c_re, c_im), (s_re, s_im)) in enumerate(zip(west(p, 0, at), west(p, 1, at))):
                t_re, t_im = jnp.where(edge, 0.0, s_re), jnp.where(edge, 0.0, s_im)
                u_re, u_im = c_re + t_im, c_im - t_re
                v_re, v_im = jnp.where(edge, s_re, c_re - t_im), jnp.where(edge, s_im, c_im + t_re)
                for i, (w_re, w_im) in ((2 * e, (u_re, u_im)), (2 * e + 1, (v_re, v_im))):
                    square = w_re * w_re + w_im * w_im
                    power[i] = square if power[i] is None else power[i] + square
        peak = power[0]
        for i, square in enumerate(power):
            power_ref[at : at + SLAB, i * half : (i + 1) * half] = square
            peak = jnp.maximum(peak, square)
        peak_ref[at : at + SLAB] = peak
    most = jnp.maximum(jnp.max(peak_ref[...], axis=1, keepdims=True), 1e-30)
    level = jnp.ceil(jnp.log2(most) * STEPS) + 1.0
    scale = LEVELS * jnp.exp2(level * (-1.0 / STEPS))
    for at in range(0, chans, SLAB):
        factor = jnp.broadcast_to(scale[at : at + SLAB], (SLAB, half))
        for i in range(2 * CYL):
            lanes = slice(i * half, (i + 1) * half)
            code = (power_ref[at : at + SLAB, lanes] * factor + (ROUND - HALF)) - ROUND
            high = ((code * (1.0 / 256.0) - (0.5 - 1.0 / 512.0) + ROUND) - ROUND) * 256.0
            high_ref[at : at + SLAB, lanes] = high.astype(jnp.bfloat16)
            low_ref[at : at + SLAB, lanes] = (code - high).astype(jnp.bfloat16)
    parts = [
        lax.dot_general(
            pick_ref[...], ref[...], (((1,), (1,)), ((), ())), preferred_element_type=jnp.float32
        )
        for ref in (high_ref, low_ref)
    ]
    for group in range(BEAMS // 8):
        rows = slice(8 * group, 8 * group + 8)
        total = parts[0][rows] + parts[1][rows]
        both = jnp.concatenate([total[:, : chans // 2], total[:, chans // 2 :]], axis=0)
        out_ref[group, pl.ds(pl.multiple_of(16 * t, 16), 16), :] = both.astype(jnp.int32).astype(jnp.int16)
    levels = jnp.transpose(jnp.broadcast_to(level, (chans, 128)))[:1]
    unit_ref[pl.ds(2 * t, 1), :] = levels[:, : chans // 2]
    unit_ref[pl.ds(2 * t + 1, 1), :] = levels[:, chans // 2 :]

    @pl.when(t == pl.num_programs(1) - 1)
    def _():
        levels = jnp.concatenate([unit_ref[...], jnp.zeros_like(unit_ref)], axis=0)
        levels = levels.astype(jnp.int32).astype(jnp.int16)
        groups = out_ref.shape[0]
        out_ref[:, SAMPLE_ROWS:, :] = jnp.broadcast_to(
            levels[None, : out_ref.shape[1] - SAMPLE_ROWS], (groups, out_ref.shape[1] - SAMPLE_ROWS, chans // 2)
        )


def form_beams(voltages, slot_feed, table, first, second, pick, deepest, chunk, chans):
    samples = voltages.shape[1]
    block = 256
    steps = chans // block
    base = chunk * steps
    groups = BEAMS // 8
    whole = pl.BlockSpec(memory_space=pltpu.VMEM)
    return pl.pallas_call(
        form_kernel,
        grid=(steps, samples),
        in_specs=[
            pl.BlockSpec((block, 1, 2, FEEDS), lambda c, t: (base + c, t, 0, 0)),
            whole,
            whole,
            whole,
            whole,
            whole,
            pl.BlockSpec(memory_space=pltpu.SMEM),
        ],
        out_specs=pl.BlockSpec((groups, ROWS, block // 2), lambda c, t: (0, 0, c)),
        out_shape=jax.ShapeDtypeStruct((groups, ROWS, chans // 2), jnp.int16),
        scratch_shapes=[
            pltpu.VMEM((FEEDS // 128, 2 * block, 128), jnp.float32),
            pltpu.VMEM((8, block // 2), jnp.float32),
            pltpu.VMEM((block, BEAMS), jnp.float32),
            pltpu.VMEM((block, 128), jnp.float32),
            pltpu.VMEM((block, BEAMS), jnp.bfloat16),
            pltpu.VMEM((block, BEAMS), jnp.bfloat16),
        ],
        compiler_params=pltpu.CompilerParams(vmem_limit_bytes=56 * 2**20),
        cost_estimate=pl.CostEstimate(
            flops=int(2 * chans * samples * (2 * FEEDS * 512 + 2 * 8 * 512 * 256 + 2 * BEAMS * BEAMS)),
            bytes_accessed=chans * samples * 2 * FEEDS * 4,
            transcendentals=0,
        ),
        name="form_beams",
    )(voltages, slot_feed, table, first, second, pick, deepest)


def normal_rows(held_ref, at):
    shards = held_ref.shape[0] // TOGETHER
    samples = TIME // shards
    half = held_ref.shape[-1]
    parts = []
    for shard in range(shards):
        block = held_ref.at[at * shards + shard]
        level = block[SAMPLE_ROWS:, :].astype(jnp.float32)
        unit = jnp.exp2(level * (1.0 / STEPS)) * (0.25 / LEVELS)
        for t in range(samples):
            code = block[16 * t : 16 * t + 16, :].astype(jnp.float32) + HALF
            ends = [
                code[8 * h : 8 * h + 8] * unit[2 * t + h : 2 * t + h + 1] for h in range(2)
            ]
            parts.append(jnp.concatenate(ends, axis=1))
    average = functools.reduce(jnp.add, parts) / TIME
    rows = [
        jnp.concatenate([parts[i] - average, parts[i + 1] - average], axis=0).astype(jnp.bfloat16)
        for i in range(0, TIME, 2)
    ]
    return jnp.concatenate(rows, axis=0)


def add_delayed(held_ref, lag_ref, trial_ref, total_ref):
    normals, delays = [], []
    for at in range(TOGETHER):
        normals.append(normal_rows(held_ref, at))
        lag = column_of(lag_ref[at])
        delays.append(jnp.floor(lag * trial_ref[...] * (1.0 / QUANT)).astype(jnp.bfloat16))
    normal = jnp.concatenate(normals, axis=1)
    delay = jnp.concatenate(delays, axis=0)
    one, zero = jnp.ones((), jnp.bfloat16), jnp.zeros((), jnp.bfloat16)
    for k in range(MAXD + 1):
        onehot = jnp.where(delay == jnp.bfloat16(k), one, zero)
        keep = TIME * 8 - 8 * k
        rows = -(-keep // 16) * 16
        part = jnp.dot(normal[:rows], onehot, preferred_element_type=jnp.float32)
        total_ref[8 * k :, :] += part[:keep]


def sum_kernel(held_ref, lag_ref, trial_ref, total_ref):
    @pl.when(pl.program_id(0) == 0)
    def _():
        total_ref[...] = jnp.zeros_like(total_ref)

    add_delayed(held_ref, lag_ref, trial_ref, total_ref)


def share_kernel(
    held_ref, lag_ref, trial_ref, before_ref, out_ref, total_ref, landed_ref, send_sem, recv_sem
):
    shards, rows = landed_ref.shape[0], landed_ref.shape[1]
    step = pl.program_id(0)
    me = lax.axis_index("tm")
    barrier = pltpu.get_barrier_semaphore()

    def device(other):
        return (lax.axis_index("sub"), other)

    def copy(i):
        other = lax.rem(me + i, shards)
        return pltpu.make_async_remote_copy(
            src_ref=total_ref.at[pl.ds(pl.multiple_of(other * rows, 8), rows), :],
            dst_ref=landed_ref.at[me],
            send_sem=send_sem.at[i],
            recv_sem=recv_sem.at[i],
            device_id=device(other),
            device_id_type=pl.DeviceIdType.MESH,
        )

    @pl.when(step == 0)
    def _():
        for i in range(1, shards):
            pl.semaphore_signal(
                barrier, inc=1, device_id=device(lax.rem(me + i, shards)), device_id_type=pl.DeviceIdType.MESH
            )
        total_ref[...] = before_ref[...]

    add_delayed(held_ref, lag_ref, trial_ref, total_ref)

    @pl.when(step == pl.num_programs(0) - 1)
    def _():
        pl.semaphore_wait(barrier, shards - 1)
        copies = [copy(i) for i in range(1, shards)]
        for each in copies:
            each.start()
        landed_ref[me] = total_ref[pl.ds(pl.multiple_of(me * rows, 8), rows), :]
        for each in copies:
            each.wait()
        scale = 1.0 / math.sqrt(CHANNELS)
        for shard in range(shards):
            for t in range(rows // 8):
                out_ref[t, 8 * shard : 8 * shard + 8, :] = landed_ref[shard, 8 * t : 8 * t + 8, :] * scale


def sum_delays(held, lags, trials, before):
    chans = 2 * held.shape[-1]
    subs = lags.shape[0]
    shards = held.shape[0] // subs
    rows = TIME * 8
    whole = pl.BlockSpec(memory_space=pltpu.VMEM)
    in_specs = [
        pl.BlockSpec((TOGETHER * shards, ROWS, chans // 2), lambda s: (s, 0, 0)),
        pl.BlockSpec((TOGETHER, 1, chans), lambda s: (s, 0, 0)),
        whole,
    ]
    cost = pl.CostEstimate(
        flops=2 * subs * chans * rows * NDM * 7,
        bytes_accessed=subs * chans * rows * 2,
        transcendentals=0,
    )
    if before is None:
        return pl.pallas_call(
            sum_kernel,
            grid=(subs // TOGETHER,),
            in_specs=in_specs,
            out_specs=pl.BlockSpec((rows, NDM), lambda s: (0, 0)),
            out_shape=jax.ShapeDtypeStruct((rows, NDM), jnp.float32),
            compiler_params=pltpu.CompilerParams(vmem_limit_bytes=56 * 2**20),
            cost_estimate=cost,
            name="sum_delays",
        )(held, lags, trials)
    samples = TIME // shards
    return pl.pallas_call(
        share_kernel,
        grid=(subs // TOGETHER,),
        in_specs=in_specs + [whole],
        out_specs=pl.BlockSpec((samples, 8 * shards, NDM), lambda s: (0, 0, 0)),
        out_shape=jax.ShapeDtypeStruct((samples, 8 * shards, NDM), jnp.float32),
        scratch_shapes=[
            pltpu.VMEM((rows, NDM), jnp.float32),
            pltpu.VMEM((shards, rows // shards, NDM), jnp.float32),
            pltpu.SemaphoreType.DMA((shards,)),
            pltpu.SemaphoreType.DMA((shards,)),
        ],
        compiler_params=pltpu.CompilerParams(
            vmem_limit_bytes=56 * 2**20, collective_id=0, has_side_effects=True
        ),
        cost_estimate=cost,
        name="sum_and_share",
    )(held, lags, trials, before)


def per_device(voltages, slot_feed, chan_lag, trial_dm, beam_order):
    subs = lax.axis_size("sub")
    table = jnp.asarray(half_table())
    lags = chan_lag.astype(jnp.float32).reshape(subs, CHUNKS, -1)
    trials = trial_dm.astype(jnp.float32).reshape(1, NDM)
    feeds = slot_feed.reshape(1, FEEDS)
    order = beam_order.reshape(1, BEAMS)
    chans = voltages.shape[0] // CHUNKS
    total = None
    first, second, pick, deepest = route(feeds, order, table)
    for chunk in range(CHUNKS):
        formed = form_beams(voltages, feeds, table, first, second, pick, deepest, chunk, chans)
        held = lax.all_to_all(formed, AXES, 0, 0)
        total = sum_delays(held, lags[:, chunk : chunk + 1], trials, total)
    return total.transpose(1, 0, 2)


def solution(mesh):
    placed = (P("sub", "tm", None, None), P(), P(), P(), P())
    return jax.shard_map(
        per_device, mesh=mesh, in_specs=placed, out_specs=P("sub", "tm", None), check_vma=False
    )
```

```python
import functools
import math

import jax
import jax.numpy as jnp
import ml_dtypes
import numpy as np
from jax import lax
from jax.experimental import pallas as pl
from jax.experimental.pallas import tpu as pltpu
from jax.sharding import PartitionSpec as P

NS = 256
CYL = 4
POL = 2
CHANNELS = 8192
NDM = 512
MAXD = 6
QUANT = 2796202
FEEDS = 2048
BEAMS = 1024
TIME = 24
CHUNKS = 2
LEVELS = 65535.0
HALF = 32768.0
STEPS = 256.0
ROUND = 12582912.0
SLAB = 32
TOGETHER = 8
GROUPS = 8
ROOM = 64
SAMPLE_ROWS = 48
ROWS = 56
AXES = ("sub", "tm")


def half_table():
    n = np.arange(NS)[:, None]
    m = np.arange(NS // 2)[None, :]
    angles = (n * m % NS) * (2.0 * math.pi / NS)
    cosine = np.cos(angles) / math.sqrt(NS)
    sine = np.sin(angles) / math.sqrt(NS)
    sine[:, 0] = np.cos((np.arange(NS) * (NS // 2) % NS) * (2.0 * math.pi / NS)) / math.sqrt(NS)
    return np.concatenate([cosine, sine], axis=1).astype(np.float32).astype(ml_dtypes.bfloat16)


def as_onehot(hit):
    return hit.astype(jnp.float32).astype(jnp.bfloat16)


def column_of(row):
    return jnp.transpose(jnp.broadcast_to(row, (8, row.shape[1])))[:, :1]


def route(feed_ref, order_ref, table_ref, first_ref, second_ref, pick_ref, deepest_ref):
    deepest = jnp.zeros((), jnp.int32)
    codes = []
    above = lax.broadcasted_iota(jnp.int32, (NS, NS), 0) < lax.broadcasted_iota(jnp.int32, (NS, NS), 1)
    for d in range(GROUPS):
        block = feed_ref[:, d * NS : (d + 1) * NS] // NS
        same = (column_of(block) == block) & above
        rank = jnp.sum(same.astype(jnp.float32), axis=0, keepdims=True).astype(jnp.int32)
        deepest = jnp.maximum(deepest, jnp.max(rank))
        odd = block % 2
        flip = odd if d % 2 == 0 else 1 - odd
        codes.append((jnp.where(odd == 0, d, d ^ 1)) * ROOM + rank)
        place = block // 2 * (2 * ROOM) + flip * ROOM + rank
        hit = lax.broadcasted_iota(jnp.int32, (GROUPS * ROOM, NS), 0) == place
        second_ref[d] = jnp.dot(
            as_onehot(hit), table_ref[...], preferred_element_type=jnp.float32
        ).astype(jnp.bfloat16)
    code = jnp.concatenate(codes, axis=1).astype(jnp.float32)
    for b in range(GROUPS):
        feeds = lax.broadcasted_iota(jnp.int32, (NS, FEEDS), 0) + b * NS
        mine = jnp.sum(jnp.where(feeds == feed_ref[...], code, 0.0), axis=1, keepdims=True)
        lanes = lax.broadcasted_iota(jnp.int32, (NS, GROUPS * ROOM), 1)
        first_ref[b] = as_onehot(mine.astype(jnp.int32) == lanes)
    north = order_ref[...] % NS
    wanted = order_ref[...] - north + jnp.where(north <= NS // 2, north, NS + NS // 2 - north)
    pick_ref[...] = as_onehot(column_of(wanted) == lax.broadcasted_iota(jnp.int32, (BEAMS, BEAMS), 1))
    deepest_ref[0] = deepest


def form_kernel(
    volt_ref, feed_ref, order_ref, table_ref, out_ref,
    grid_ref, unit_ref, power_ref, peak_ref, high_ref, low_ref, first_ref, second_ref, pick_ref, deepest_ref,
):
    @pl.when((pl.program_id(0) == 0) & (pl.program_id(1) == 0))
    def _():
        route(feed_ref, order_ref, table_ref, first_ref, second_ref, pick_ref, deepest_ref)

    chans = volt_ref.shape[0]
    half = NS // 2
    t = pl.program_id(1)

    @pl.when(t == 0)
    def _():
        unit_ref[...] = jnp.zeros_like(unit_ref)

    @pl.when(deepest_ref[0] < ROOM)
    def _():
        rows = volt_ref[:, 0].reshape(2 * chans, FEEDS)
        low_half = lax.broadcasted_iota(jnp.int32, (2 * chans, half), 1) < ROOM
        pieces = [[] for _ in range(GROUPS)]
        for q in range(GROUPS // 2):
            ways = []
            for b in (2 * q, 2 * q + 1):
                way = jnp.dot(
                    rows[:, b * NS : (b + 1) * NS], first_ref[b], preferred_element_type=jnp.float32
                )
                ways.append(way)
            for v in range(GROUPS // 2):
                one = ways[0][:, v * half : (v + 1) * half]
                two = ways[1][:, v * half : (v + 1) * half]
                pieces[2 * v].append(jnp.where(low_half, one, two).astype(jnp.bfloat16))
                pieces[2 * v + 1].append(jnp.where(low_half, two, one).astype(jnp.bfloat16))
        for d in range(GROUPS):
            wave = jnp.dot(
                jnp.concatenate(pieces[d], axis=1), second_ref[d], preferred_element_type=jnp.float32
            )
            grid_ref[2 * d] = wave[:, :half]
            grid_ref[2 * d + 1] = wave[:, half:]

    @pl.when(deepest_ref[0] >= ROOM)
    def _():
        rows = volt_ref[:, 0].reshape(2 * chans, FEEDS)
        for d in range(GROUPS):
            feeds = lax.broadcasted_iota(jnp.int32, (FEEDS, NS), 0)
            place = as_onehot(feeds == feed_ref[:, d * NS : (d + 1) * NS])
            slots = jnp.dot(rows, place, preferred_element_type=jnp.float32).astype(jnp.bfloat16)
            wave = jnp.dot(slots, table_ref[...], preferred_element_type=jnp.float32)
            grid_ref[2 * d] = wave[:, :half]
            grid_ref[2 * d + 1] = wave[:, half:]

    edge = lax.broadcasted_iota(jnp.int32, (SLAB, half), 1) == 0

    def west(p, part, at):
        re, im = [], []
        for y in range(CYL):
            tile = 2 * (p * CYL + y) + part
            re.append(grid_ref[tile, pl.ds(2 * at, SLAB, stride=2), :])
            im.append(grid_ref[tile, pl.ds(2 * at + 1, SLAB, stride=2), :])
        a_re, a_im = re[0] + re[2], im[0] + im[2]
        b_re, b_im = re[0] - re[2], im[0] - im[2]
        c_re, c_im = re[1] + re[3], im[1] + im[3]
        d_re, d_im = re[1] - re[3], im[1] - im[3]
        return [
            (a_re + c_re, a_im + c_im),
            (b_re + d_im, b_im - d_re),
            (a_re - c_re, a_im - c_im),
            (b_re - d_im, b_im + d_re),
        ]

    for at in range(0, chans, SLAB):
        power = [None] * (2 * CYL)
        for p in range(POL):
            for e, ((c_re, c_im), (s_re, s_im)) in enumerate(zip(west(p, 0, at), west(p, 1, at))):
                t_re, t_im = jnp.where(edge, 0.0, s_re), jnp.where(edge, 0.0, s_im)
                u_re, u_im = c_re + t_im, c_im - t_re
                v_re, v_im = jnp.where(edge, s_re, c_re - t_im), jnp.where(edge, s_im, c_im + t_re)
                for i, (w_re, w_im) in ((2 * e, (u_re, u_im)), (2 * e + 1, (v_re, v_im))):
                    square = w_re * w_re + w_im * w_im
                    power[i] = square if power[i] is None else power[i] + square
        peak = power[0]
        for i, square in enumerate(power):
            power_ref[at : at + SLAB, i * half : (i + 1) * half] = square
            peak = jnp.maximum(peak, square)
        peak_ref[at : at + SLAB] = peak
    most = jnp.maximum(jnp.max(peak_ref[...], axis=1, keepdims=True), 1e-30)
    level = jnp.ceil(jnp.log2(most) * STEPS) + 1.0
    scale = LEVELS * jnp.exp2(level * (-1.0 / STEPS))
    for at in range(0, chans, SLAB):
        factor = jnp.broadcast_to(scale[at : at + SLAB], (SLAB, half))
        for i in range(2 * CYL):
            lanes = slice(i * half, (i + 1) * half)
            code = (power_ref[at : at + SLAB, lanes] * factor + (ROUND - HALF)) - ROUND
            high = ((code * (1.0 / 256.0) - (0.5 - 1.0 / 512.0) + ROUND) - ROUND) * 256.0
            high_ref[at : at + SLAB, lanes] = high.astype(jnp.bfloat16)
            low_ref[at : at + SLAB, lanes] = (code - high).astype(jnp.bfloat16)
    parts = [
        lax.dot_general(
            pick_ref[...], ref[...], (((1,), (1,)), ((), ())), preferred_element_type=jnp.float32
        )
        for ref in (high_ref, low_ref)
    ]
    for group in range(BEAMS // 8):
        rows = slice(8 * group, 8 * group + 8)
        total = parts[0][rows] + parts[1][rows]
        both = jnp.concatenate([total[:, : chans // 2], total[:, chans // 2 :]], axis=0)
        out_ref[group, pl.ds(pl.multiple_of(16 * t, 16), 16), :] = both.astype(jnp.int32).astype(jnp.int16)
    levels = jnp.transpose(jnp.broadcast_to(level, (chans, 128)))[:1]
    unit_ref[pl.ds(2 * t, 1), :] = levels[:, : chans // 2]
    unit_ref[pl.ds(2 * t + 1, 1), :] = levels[:, chans // 2 :]

    @pl.when(t == pl.num_programs(1) - 1)
    def _():
        levels = jnp.concatenate([unit_ref[...], jnp.zeros_like(unit_ref)], axis=0)
        levels = levels.astype(jnp.int32).astype(jnp.int16)
        groups = out_ref.shape[0]
        out_ref[:, SAMPLE_ROWS:, :] = jnp.broadcast_to(
            levels[None, : out_ref.shape[1] - SAMPLE_ROWS], (groups, out_ref.shape[1] - SAMPLE_ROWS, chans // 2)
        )


def form_beams(voltages, slot_feed, beam_order, table, chunk, chans):
    samples = voltages.shape[1]
    block = 256
    steps = chans // block
    base = chunk * steps
    groups = BEAMS // 8
    whole = pl.BlockSpec(memory_space=pltpu.VMEM)
    return pl.pallas_call(
        form_kernel,
        grid=(steps, samples),
        in_specs=[
            pl.BlockSpec((block, 1, 2, FEEDS), lambda c, t: (base + c, t, 0, 0)),
            whole,
            whole,
            whole,
        ],
        out_specs=pl.BlockSpec((groups, ROWS, block // 2), lambda c, t: (0, 0, c)),
        out_shape=jax.ShapeDtypeStruct((groups, ROWS, chans // 2), jnp.int16),
        scratch_shapes=[
            pltpu.VMEM((FEEDS // 128, 2 * block, 128), jnp.float32),
            pltpu.VMEM((8, block // 2), jnp.float32),
            pltpu.VMEM((block, BEAMS), jnp.float32),
            pltpu.VMEM((block, 128), jnp.float32),
            pltpu.VMEM((block, BEAMS), jnp.bfloat16),
            pltpu.VMEM((block, BEAMS), jnp.bfloat16),
            pltpu.VMEM((GROUPS, NS, GROUPS * ROOM), jnp.bfloat16),
            pltpu.VMEM((GROUPS, GROUPS * ROOM, NS), jnp.bfloat16),
            pltpu.VMEM((BEAMS, BEAMS), jnp.bfloat16),
            pltpu.SMEM((1,), jnp.int32),
        ],
        compiler_params=pltpu.CompilerParams(vmem_limit_bytes=56 * 2**20),
        cost_estimate=pl.CostEstimate(
            flops=int(2 * chans * samples * (2 * FEEDS * 512 + 2 * 8 * 512 * 256 + 2 * BEAMS * BEAMS)),
            bytes_accessed=chans * samples * 2 * FEEDS * 4,
            transcendentals=0,
        ),
        name="form_beams",
    )(voltages, slot_feed, beam_order, table)


def normal_rows(held_ref, at):
    shards = held_ref.shape[0] // TOGETHER
    samples = TIME // shards
    half = held_ref.shape[-1]
    parts = []
    for shard in range(shards):
        block = held_ref.at[at * shards + shard]
        level = block[SAMPLE_ROWS:, :].astype(jnp.float32)
        unit = jnp.exp2(level * (1.0 / STEPS)) * (0.25 / LEVELS)
        for t in range(samples):
            code = block[16 * t : 16 * t + 16, :].astype(jnp.float32) + HALF
            ends = [
                code[8 * h : 8 * h + 8] * unit[2 * t + h : 2 * t + h + 1] for h in range(2)
            ]
            parts.append(jnp.concatenate(ends, axis=1))
    average = functools.reduce(jnp.add, parts) / TIME
    rows = [
        jnp.concatenate([parts[i] - average, parts[i + 1] - average], axis=0).astype(jnp.bfloat16)
        for i in range(0, TIME, 2)
    ]
    return jnp.concatenate(rows, axis=0)


def gathered_rows(held_ref, lag_ref, trial_ref):
    normals, delays = [], []
    for at in range(TOGETHER):
        normals.append(normal_rows(held_ref, at))
        lag = column_of(lag_ref[at])
        delays.append(jnp.floor(lag * trial_ref[...] * (1.0 / QUANT)).astype(jnp.bfloat16))
    return jnp.concatenate(normals, axis=1), jnp.concatenate(delays, axis=0)


def add_delayed(normal, delay, total_ref, lanes):
    one, zero = jnp.ones((), jnp.bfloat16), jnp.zeros((), jnp.bfloat16)
    for k in range(MAXD + 1):
        onehot = jnp.where(delay[:, lanes] == jnp.bfloat16(k), one, zero)
        keep = TIME * 8 - 8 * k
        rows = -(-keep // 16) * 16
        part = jnp.dot(normal[:rows], onehot, preferred_element_type=jnp.float32)
        total_ref[8 * k :, lanes] += part[:keep]


def sum_kernel(held_ref, lag_ref, trial_ref, total_ref):
    @pl.when(pl.program_id(0) == 0)
    def _():
        total_ref[...] = jnp.zeros_like(total_ref)

    normal, delay = gathered_rows(held_ref, lag_ref, trial_ref)
    add_delayed(normal, delay, total_ref, slice(0, NDM))


def share_kernel(
    held_ref, lag_ref, trial_ref, before_ref, out_ref, total_ref, landed_ref, send_sem, recv_sem
):
    shards, rows = landed_ref.shape[0], landed_ref.shape[1]
    step = pl.program_id(0)
    me = lax.axis_index("tm")
    barrier = pltpu.get_barrier_semaphore()

    def device(other):
        return (lax.axis_index("sub"), other)

    def copy(i, h):
        other = lax.rem(me + i, shards)
        lanes = slice(h * (NDM // 2), (h + 1) * (NDM // 2))
        return pltpu.make_async_remote_copy(
            src_ref=total_ref.at[pl.ds(pl.multiple_of(other * rows, 8), rows), lanes],
            dst_ref=landed_ref.at[me, :, lanes],
            send_sem=send_sem.at[h, i],
            recv_sem=recv_sem.at[h, i],
            device_id=device(other),
            device_id_type=pl.DeviceIdType.MESH,
        )

    @pl.when(step == 0)
    def _():
        for i in range(1, shards):
            pl.semaphore_signal(
                barrier, inc=1, device_id=device(lax.rem(me + i, shards)), device_id_type=pl.DeviceIdType.MESH
            )
        total_ref[...] = before_ref[...]

    normal, delay = gathered_rows(held_ref, lag_ref, trial_ref)
    add_delayed(normal, delay, total_ref, slice(0, NDM // 2))

    @pl.when(step == pl.num_programs(0) - 1)
    def _():
        pl.semaphore_wait(barrier, shards - 1)
        for i in range(1, shards):
            copy(i, 0).start()

    add_delayed(normal, delay, total_ref, slice(NDM // 2, NDM))

    @pl.when(step == pl.num_programs(0) - 1)
    def _():
        for i in range(1, shards):
            copy(i, 1).start()
        landed_ref[me] = total_ref[pl.ds(pl.multiple_of(me * rows, 8), rows), :]
        for h in range(2):
            for i in range(1, shards):
                copy(i, h).wait()
        scale = 1.0 / math.sqrt(CHANNELS)
        for shard in range(shards):
            for t in range(rows // 8):
                out_ref[t, 8 * shard : 8 * shard + 8, :] = landed_ref[shard, 8 * t : 8 * t + 8, :] * scale


def sum_delays(held, lags, trials, before):
    chans = 2 * held.shape[-1]
    subs = lags.shape[0]
    shards = held.shape[0] // subs
    rows = TIME * 8
    whole = pl.BlockSpec(memory_space=pltpu.VMEM)
    in_specs = [
        pl.BlockSpec((TOGETHER * shards, ROWS, chans // 2), lambda s: (s, 0, 0)),
        pl.BlockSpec((TOGETHER, 1, chans), lambda s: (s, 0, 0)),
        whole,
    ]
    cost = pl.CostEstimate(
        flops=2 * subs * chans * rows * NDM * 7,
        bytes_accessed=subs * chans * rows * 2,
        transcendentals=0,
    )
    if before is None:
        return pl.pallas_call(
            sum_kernel,
            grid=(subs // TOGETHER,),
            in_specs=in_specs,
            out_specs=pl.BlockSpec((rows, NDM), lambda s: (0, 0)),
            out_shape=jax.ShapeDtypeStruct((rows, NDM), jnp.float32),
            compiler_params=pltpu.CompilerParams(vmem_limit_bytes=56 * 2**20),
            cost_estimate=cost,
            name="sum_delays",
        )(held, lags, trials)
    samples = TIME // shards
    return pl.pallas_call(
        share_kernel,
        grid=(subs // TOGETHER,),
        in_specs=in_specs + [whole],
        out_specs=pl.BlockSpec((samples, 8 * shards, NDM), lambda s: (0, 0, 0)),
        out_shape=jax.ShapeDtypeStruct((samples, 8 * shards, NDM), jnp.float32),
        scratch_shapes=[
            pltpu.VMEM((rows, NDM), jnp.float32),
            pltpu.VMEM((shards, rows // shards, NDM), jnp.float32),
            pltpu.SemaphoreType.DMA((2, shards)),
            pltpu.SemaphoreType.DMA((2, shards)),
        ],
        compiler_params=pltpu.CompilerParams(
            vmem_limit_bytes=56 * 2**20, collective_id=0, has_side_effects=True
        ),
        cost_estimate=cost,
        name="sum_and_share",
    )(held, lags, trials, before)


def per_device(voltages, slot_feed, chan_lag, trial_dm, beam_order):
    subs = lax.axis_size("sub")
    table = jnp.asarray(half_table())
    lags = chan_lag.astype(jnp.float32).reshape(subs, CHUNKS, -1)
    trials = trial_dm.astype(jnp.float32).reshape(1, NDM)
    feeds = slot_feed.reshape(1, FEEDS)
    order = beam_order.reshape(1, BEAMS)
    chans = voltages.shape[0] // CHUNKS
    total = None
    for chunk in range(CHUNKS):
        formed = form_beams(voltages, feeds, order, table, chunk, chans)
        held = lax.all_to_all(formed, AXES, 0, 0)
        total = sum_delays(held, lags[:, chunk : chunk + 1], trials, total)
    return total.transpose(1, 0, 2)


def solution(mesh):
    placed = (P("sub", "tm", None, None), P(), P(), P(), P())
    return jax.shard_map(
        per_device, mesh=mesh, in_specs=placed, out_specs=P("sub", "tm", None), check_vma=False
    )
```

```python
import functools
import math

import jax
import jax.numpy as jnp
import ml_dtypes
import numpy as np
from jax import lax
from jax.experimental import pallas as pl
from jax.experimental.pallas import tpu as pltpu
from jax.sharding import PartitionSpec as P

NS = 256
CYL = 4
POL = 2
CHANNELS = 8192
NDM = 512
MAXD = 6
QUANT = 2796202
FEEDS = 2048
BEAMS = 1024
TIME = 24
CHUNKS = 2
LEVELS = 65535.0
HALF = 32768.0
STEPS = 256.0
ROUND = 12582912.0
TOGETHER = 8
GROUPS = 8
ROOM = 64
SAMPLE_ROWS = 48
ROWS = 56
AXES = ("sub", "tm")


def half_table():
    n = np.arange(NS)[:, None]
    m = np.arange(NS // 2)[None, :]
    angles = (n * m % NS) * (2.0 * math.pi / NS)
    cosine = np.cos(angles) / math.sqrt(NS)
    sine = np.sin(angles) / math.sqrt(NS)
    sine[:, 0] = np.cos((np.arange(NS) * (NS // 2) % NS) * (2.0 * math.pi / NS)) / math.sqrt(NS)
    return np.concatenate([cosine, sine], axis=1).astype(np.float32).astype(ml_dtypes.bfloat16)


def as_onehot(hit):
    return hit.astype(jnp.float32).astype(jnp.bfloat16)


def column_of(row):
    return jnp.transpose(jnp.broadcast_to(row, (8, row.shape[1])))[:, :1]


def route_kernel(feed_ref, order_ref, table_ref, first_ref, second_ref, pick_ref, deepest_ref):
    deepest = jnp.zeros((), jnp.int32)
    codes = []
    above = lax.broadcasted_iota(jnp.int32, (NS, NS), 0) < lax.broadcasted_iota(jnp.int32, (NS, NS), 1)
    for d in range(GROUPS):
        block = feed_ref[:, d * NS : (d + 1) * NS] // NS
        same = (column_of(block) == block) & above
        rank = jnp.sum(same.astype(jnp.float32), axis=0, keepdims=True).astype(jnp.int32)
        deepest = jnp.maximum(deepest, jnp.max(rank))
        odd = block % 2
        flip = odd if d % 2 == 0 else 1 - odd
        codes.append((jnp.where(odd == 0, d, d ^ 1)) * ROOM + rank)
        place = block // 2 * (2 * ROOM) + flip * ROOM + rank
        hit = lax.broadcasted_iota(jnp.int32, (GROUPS * ROOM, NS), 0) == place
        second_ref[d] = jnp.dot(
            as_onehot(hit), table_ref[...], preferred_element_type=jnp.float32
        ).astype(jnp.bfloat16)
    code = jnp.concatenate(codes, axis=1).astype(jnp.float32)
    for b in range(GROUPS):
        feeds = lax.broadcasted_iota(jnp.int32, (NS, FEEDS), 0) + b * NS
        mine = jnp.sum(jnp.where(feeds == feed_ref[...], code, 0.0), axis=1, keepdims=True)
        lanes = lax.broadcasted_iota(jnp.int32, (NS, GROUPS * ROOM), 1)
        first_ref[b] = as_onehot(mine.astype(jnp.int32) == lanes)
    north = order_ref[...] % NS
    wanted = order_ref[...] - north + jnp.where(north <= NS // 2, north, NS + NS // 2 - north)
    pick_ref[...] = as_onehot(column_of(wanted) == lax.broadcasted_iota(jnp.int32, (BEAMS, BEAMS), 1))
    deepest_ref[0] = deepest


def route(slot_feed, beam_order, table):
    whole = pl.BlockSpec(memory_space=pltpu.VMEM)
    return pl.pallas_call(
        route_kernel,
        in_specs=[whole, whole, whole],
        out_specs=[whole, whole, whole, pl.BlockSpec(memory_space=pltpu.SMEM)],
        out_shape=[
            jax.ShapeDtypeStruct((GROUPS, NS, GROUPS * ROOM), jnp.bfloat16),
            jax.ShapeDtypeStruct((GROUPS, GROUPS * ROOM, NS), jnp.bfloat16),
            jax.ShapeDtypeStruct((BEAMS, BEAMS), jnp.bfloat16),
            jax.ShapeDtypeStruct((1,), jnp.int32),
        ],
        compiler_params=pltpu.CompilerParams(vmem_limit_bytes=56 * 2**20),
        name="route",
    )(slot_feed, beam_order, table)


def form_kernel(
    volt_ref, feed_ref, table_ref, first_ref, second_ref, pick_ref, deepest_ref, out_ref, grid_ref, unit_ref
):
    chans = volt_ref.shape[0]
    half = NS // 2
    t = pl.program_id(1)

    @pl.when(t == 0)
    def _():
        unit_ref[...] = jnp.zeros_like(unit_ref)

    def finish():
        edge = lax.broadcasted_iota(jnp.int32, (chans, half), 1) == 0

        def west(p, part):
            re, im = [], []
            for y in range(CYL):
                tile = 2 * (p * CYL + y) + part
                re.append(grid_ref[tile, pl.ds(0, chans, stride=2), :])
                im.append(grid_ref[tile, pl.ds(1, chans, stride=2), :])
            a_re, a_im = re[0] + re[2], im[0] + im[2]
            b_re, b_im = re[0] - re[2], im[0] - im[2]
            c_re, c_im = re[1] + re[3], im[1] + im[3]
            d_re, d_im = re[1] - re[3], im[1] - im[3]
            return [
                (a_re + c_re, a_im + c_im),
                (b_re + d_im, b_im - d_re),
                (a_re - c_re, a_im - c_im),
                (b_re - d_im, b_im + d_re),
            ]

        power = [None] * (2 * CYL)
        for p in range(POL):
            for e, ((c_re, c_im), (s_re, s_im)) in enumerate(zip(west(p, 0), west(p, 1))):
                t_re, t_im = jnp.where(edge, 0.0, s_re), jnp.where(edge, 0.0, s_im)
                u_re, u_im = c_re + t_im, c_im - t_re
                v_re, v_im = jnp.where(edge, s_re, c_re - t_im), jnp.where(edge, s_im, c_im + t_re)
                for at, (w_re, w_im) in ((2 * e, (u_re, u_im)), (2 * e + 1, (v_re, v_im))):
                    square = w_re * w_re + w_im * w_im
                    power[at] = square if power[at] is None else power[at] + square
        power = jnp.concatenate(power, axis=1)
        most = jnp.maximum(jnp.max(power, axis=1, keepdims=True), 1e-30)
        level = jnp.ceil(jnp.log2(most) * STEPS) + 1.0
        scale = LEVELS * jnp.exp2(level * (-1.0 / STEPS))
        code = (power * scale + (ROUND - HALF)) - ROUND
        high = ((code * (1.0 / 256.0) - (0.5 - 1.0 / 512.0) + ROUND) - ROUND) * 256.0
        low = (code - high).astype(jnp.bfloat16)
        total = None
        for piece in (high.astype(jnp.bfloat16), low):
            part = lax.dot_general(
                pick_ref[...], piece, (((1,), (1,)), ((), ())), preferred_element_type=jnp.float32
            )
            total = part if total is None else total + part
        total = total.reshape(BEAMS // 8, 8, chans)
        both = jnp.concatenate([total[:, :, : chans // 2], total[:, :, chans // 2 :]], axis=1)
        out_ref[:, pl.ds(pl.multiple_of(16 * t, 16), 16), :] = both.astype(jnp.int32).astype(jnp.int16)
        levels = jnp.transpose(jnp.broadcast_to(level, (chans, 128)))[:1]
        unit_ref[pl.ds(2 * t, 1), :] = levels[:, : chans // 2]
        unit_ref[pl.ds(2 * t + 1, 1), :] = levels[:, chans // 2 :]


    @pl.when(deepest_ref[0] < ROOM)
    def _():
        rows = volt_ref[:, 0].reshape(2 * chans, FEEDS)
        low_half = lax.broadcasted_iota(jnp.int32, (2 * chans, half), 1) < ROOM
        pieces = [[] for _ in range(GROUPS)]
        for q in range(GROUPS // 2):
            ways = []
            for b in (2 * q, 2 * q + 1):
                way = jnp.dot(
                    rows[:, b * NS : (b + 1) * NS], first_ref[b], preferred_element_type=jnp.float32
                )
                ways.append(way)
            for v in range(GROUPS // 2):
                one = ways[0][:, v * half : (v + 1) * half]
                two = ways[1][:, v * half : (v + 1) * half]
                pieces[2 * v].append(jnp.where(low_half, one, two).astype(jnp.bfloat16))
                pieces[2 * v + 1].append(jnp.where(low_half, two, one).astype(jnp.bfloat16))
        for d in range(GROUPS):
            wave = jnp.dot(
                jnp.concatenate(pieces[d], axis=1), second_ref[d], preferred_element_type=jnp.float32
            )
            grid_ref[2 * d] = wave[:, :half]
            grid_ref[2 * d + 1] = wave[:, half:]
        finish()

    @pl.when(deepest_ref[0] >= ROOM)
    def _():
        rows = volt_ref[:, 0].reshape(2 * chans, FEEDS)
        for d in range(GROUPS):
            feeds = lax.broadcasted_iota(jnp.int32, (FEEDS, NS), 0)
            place = as_onehot(feeds == feed_ref[:, d * NS : (d + 1) * NS])
            slots = jnp.dot(rows, place, preferred_element_type=jnp.float32).astype(jnp.bfloat16)
            wave = jnp.dot(slots, table_ref[...], preferred_element_type=jnp.float32)
            grid_ref[2 * d] = wave[:, :half]
            grid_ref[2 * d + 1] = wave[:, half:]
        finish()

    @pl.when(t == pl.num_programs(1) - 1)
    def _():
        levels = jnp.concatenate([unit_ref[...], jnp.zeros_like(unit_ref)], axis=0)
        levels = levels.astype(jnp.int32).astype(jnp.int16)
        groups = out_ref.shape[0]
        out_ref[:, SAMPLE_ROWS:, :] = jnp.broadcast_to(
            levels[None, : out_ref.shape[1] - SAMPLE_ROWS], (groups, out_ref.shape[1] - SAMPLE_ROWS, chans // 2)
        )


def form_beams(voltages, slot_feed, table, first, second, pick, deepest, chunk, chans):
    samples = voltages.shape[1]
    block = 256
    steps = chans // block
    base = chunk * steps
    groups = BEAMS // 8
    whole = pl.BlockSpec(memory_space=pltpu.VMEM)
    return pl.pallas_call(
        form_kernel,
        grid=(steps, samples),
        in_specs=[
            pl.BlockSpec((block, 1, 2, FEEDS), lambda c, t: (base + c, t, 0, 0)),
            whole,
            whole,
            whole,
            whole,
            whole,
            pl.BlockSpec(memory_space=pltpu.SMEM),
        ],
        out_specs=pl.BlockSpec((groups, ROWS, block // 2), lambda c, t: (0, 0, c)),
        out_shape=jax.ShapeDtypeStruct((groups, ROWS, chans // 2), jnp.int16),
        scratch_shapes=[
            pltpu.VMEM((FEEDS // 128, 2 * block, 128), jnp.float32),
            pltpu.VMEM((8, block // 2), jnp.float32),
        ],
        compiler_params=pltpu.CompilerParams(vmem_limit_bytes=56 * 2**20),
        cost_estimate=pl.CostEstimate(
            flops=int(2 * chans * samples * (2 * FEEDS * 512 + 2 * 8 * 512 * 256 + 2 * BEAMS * BEAMS)),
            bytes_accessed=chans * samples * 2 * FEEDS * 4,
            transcendentals=0,
        ),
        name="form_beams",
    )(voltages, slot_feed, table, first, second, pick, deepest)


def normal_rows(held_ref, at):
    shards = held_ref.shape[0] // TOGETHER
    samples = TIME // shards
    half = held_ref.shape[-1]
    parts = []
    for shard in range(shards):
        block = held_ref.at[at * shards + shard]
        level = block[SAMPLE_ROWS:, :].astype(jnp.float32)
        unit = jnp.exp2(level * (1.0 / STEPS)) * (0.25 / LEVELS)
        for t in range(samples):
            code = block[16 * t : 16 * t + 16, :].astype(jnp.float32) + HALF
            ends = [
                code[8 * h : 8 * h + 8] * unit[2 * t + h : 2 * t + h + 1] for h in range(2)
            ]
            parts.append(jnp.concatenate(ends, axis=1))
    average = functools.reduce(jnp.add, parts) / TIME
    rows = [
        jnp.concatenate([parts[i] - average, parts[i + 1] - average], axis=0).astype(jnp.bfloat16)
        for i in range(0, TIME, 2)
    ]
    return jnp.concatenate(rows, axis=0)


def add_delayed(held_ref, lag_ref, trial_ref, total_ref):
    normals, delays = [], []
    for at in range(TOGETHER):
        normals.append(normal_rows(held_ref, at))
        lag = column_of(lag_ref[at])
        delays.append(jnp.floor(lag * trial_ref[...] * (1.0 / QUANT)).astype(jnp.bfloat16))
    normal = jnp.concatenate(normals, axis=1)
    delay = jnp.concatenate(delays, axis=0)
    one, zero = jnp.ones((), jnp.bfloat16), jnp.zeros((), jnp.bfloat16)
    for k in range(MAXD + 1):
        onehot = jnp.where(delay == jnp.bfloat16(k), one, zero)
        keep = TIME * 8 - 8 * k
        rows = -(-keep // 16) * 16
        part = jnp.dot(normal[:rows], onehot, preferred_element_type=jnp.float32)
        total_ref[8 * k :, :] += part[:keep]


def sum_kernel(held_ref, lag_ref, trial_ref, total_ref):
    @pl.when(pl.program_id(0) == 0)
    def _():
        total_ref[...] = jnp.zeros_like(total_ref)

    add_delayed(held_ref, lag_ref, trial_ref, total_ref)


def share_kernel(
    held_ref, lag_ref, trial_ref, before_ref, out_ref, total_ref, landed_ref, send_sem, recv_sem
):
    shards, rows = landed_ref.shape[0], landed_ref.shape[1]
    step = pl.program_id(0)
    me = lax.axis_index("tm")
    barrier = pltpu.get_barrier_semaphore()

    def device(other):
        return (lax.axis_index("sub"), other)

    def copy(i):
        other = lax.rem(me + i, shards)
        return pltpu.make_async_remote_copy(
            src_ref=total_ref.at[pl.ds(pl.multiple_of(other * rows, 8), rows), :],
            dst_ref=landed_ref.at[me],
            send_sem=send_sem.at[i],
            recv_sem=recv_sem.at[i],
            device_id=device(other),
            device_id_type=pl.DeviceIdType.MESH,
        )

    @pl.when(step == 0)
    def _():
        for i in range(1, shards):
            pl.semaphore_signal(
                barrier, inc=1, device_id=device(lax.rem(me + i, shards)), device_id_type=pl.DeviceIdType.MESH
            )
        total_ref[...] = before_ref[...]

    add_delayed(held_ref, lag_ref, trial_ref, total_ref)

    @pl.when(step == pl.num_programs(0) - 1)
    def _():
        pl.semaphore_wait(barrier, shards - 1)
        copies = [copy(i) for i in range(1, shards)]
        for each in copies:
            each.start()
        landed_ref[me] = total_ref[pl.ds(pl.multiple_of(me * rows, 8), rows), :]
        for each in copies:
            each.wait()
        out_ref[...] = landed_ref[...]


def sum_delays(held, lags, trials, before):
    chans = 2 * held.shape[-1]
    subs = lags.shape[0]
    shards = held.shape[0] // subs
    rows = TIME * 8
    whole = pl.BlockSpec(memory_space=pltpu.VMEM)
    in_specs = [
        pl.BlockSpec((TOGETHER * shards, ROWS, chans // 2), lambda s: (s, 0, 0)),
        pl.BlockSpec((TOGETHER, 1, chans), lambda s: (s, 0, 0)),
        whole,
    ]
    cost = pl.CostEstimate(
        flops=2 * subs * chans * rows * NDM * 7,
        bytes_accessed=subs * chans * rows * 2,
        transcendentals=0,
    )
    if before is None:
        return pl.pallas_call(
            sum_kernel,
            grid=(subs // TOGETHER,),
            in_specs=in_specs,
            out_specs=pl.BlockSpec((rows, NDM), lambda s: (0, 0)),
            out_shape=jax.ShapeDtypeStruct((rows, NDM), jnp.float32),
            compiler_params=pltpu.CompilerParams(vmem_limit_bytes=56 * 2**20),
            cost_estimate=cost,
            name="sum_delays",
        )(held, lags, trials)
    return pl.pallas_call(
        share_kernel,
        grid=(subs // TOGETHER,),
        in_specs=in_specs + [whole],
        out_specs=pl.BlockSpec((shards, rows // shards, NDM), lambda s: (0, 0, 0)),
        out_shape=jax.ShapeDtypeStruct((shards, rows // shards, NDM), jnp.float32),
        scratch_shapes=[
            pltpu.VMEM((rows, NDM), jnp.float32),
            pltpu.VMEM((shards, rows // shards, NDM), jnp.float32),
            pltpu.SemaphoreType.DMA((shards,)),
            pltpu.SemaphoreType.DMA((shards,)),
        ],
        compiler_params=pltpu.CompilerParams(
            vmem_limit_bytes=56 * 2**20, collective_id=0, has_side_effects=True
        ),
        cost_estimate=cost,
        name="sum_and_share",
    )(held, lags, trials, before)


def per_device(voltages, slot_feed, chan_lag, trial_dm, beam_order):
    subs = lax.axis_size("sub")
    table = jnp.asarray(half_table())
    lags = chan_lag.astype(jnp.float32).reshape(subs, CHUNKS, -1)
    trials = trial_dm.astype(jnp.float32).reshape(1, NDM)
    feeds = slot_feed.reshape(1, FEEDS)
    order = beam_order.reshape(1, BEAMS)
    chans = voltages.shape[0] // CHUNKS
    total = None
    first, second, pick, deepest = route(feeds, order, table)
    for chunk in range(CHUNKS):
        formed = form_beams(voltages, feeds, table, first, second, pick, deepest, chunk, chans)
        held = lax.all_to_all(formed, AXES, 0, 0)
        total = sum_delays(held, lags[:, chunk : chunk + 1], trials, total)
    shards, samples = total.shape[0], voltages.shape[1]
    parts = total.reshape(shards, samples, 8, NDM).transpose(0, 2, 1, 3)
    return parts.reshape(shards * 8, samples, NDM) * (1.0 / math.sqrt(CHANNELS))


def solution(mesh):
    placed = (P("sub", "tm", None, None), P(), P(), P(), P())
    return jax.shard_map(
        per_device, mesh=mesh, in_specs=placed, out_specs=P("sub", "tm", None), check_vma=False
    )
```

```python
import functools
import math

import jax
import jax.numpy as jnp
import ml_dtypes
import numpy as np
from jax import lax
from jax.experimental import pallas as pl
from jax.experimental.pallas import tpu as pltpu
from jax.sharding import PartitionSpec as P

NS = 256
CYL = 4
POL = 2
CHANNELS = 8192
NDM = 512
MAXD = 6
QUANT = 2796202
FEEDS = 2048
BEAMS = 1024
TIME = 24
CHUNKS = 2
LEVELS = 65535.0
HALF = 32768.0
STEPS = 256.0
ROUND = 12582912.0
TOGETHER = 8
GROUPS = 8
ROOM = 64
SAMPLE_ROWS = 48
ROWS = 56
AXES = ("sub", "tm")


def half_table():
    n = np.arange(NS)[:, None]
    m = np.arange(NS // 2)[None, :]
    angles = (n * m % NS) * (2.0 * math.pi / NS)
    cosine = np.cos(angles) / math.sqrt(NS)
    sine = np.sin(angles) / math.sqrt(NS)
    sine[:, 0] = np.cos((np.arange(NS) * (NS // 2) % NS) * (2.0 * math.pi / NS)) / math.sqrt(NS)
    return np.concatenate([cosine, sine], axis=1).astype(np.float32).astype(ml_dtypes.bfloat16)


def as_onehot(hit):
    return hit.astype(jnp.float32).astype(jnp.bfloat16)


def column_of(row):
    return jnp.transpose(jnp.broadcast_to(row, (8, row.shape[1])))[:, :1]


def route_kernel(feed_ref, order_ref, table_ref, first_ref, second_ref, pick_ref, deepest_ref):
    deepest = jnp.zeros((), jnp.int32)
    codes = []
    above = lax.broadcasted_iota(jnp.int32, (NS, NS), 0) < lax.broadcasted_iota(jnp.int32, (NS, NS), 1)
    for d in range(GROUPS):
        block = feed_ref[:, d * NS : (d + 1) * NS] // NS
        same = (column_of(block) == block) & above
        rank = jnp.sum(same.astype(jnp.float32), axis=0, keepdims=True).astype(jnp.int32)
        deepest = jnp.maximum(deepest, jnp.max(rank))
        odd = block % 2
        flip = odd if d % 2 == 0 else 1 - odd
        codes.append((jnp.where(odd == 0, d, d ^ 1)) * ROOM + rank)
        place = block // 2 * (2 * ROOM) + flip * ROOM + rank
        hit = lax.broadcasted_iota(jnp.int32, (GROUPS * ROOM, NS), 0) == place
        second_ref[d] = jnp.dot(
            as_onehot(hit), table_ref[...], preferred_element_type=jnp.float32
        ).astype(jnp.bfloat16)
    code = jnp.concatenate(codes, axis=1).astype(jnp.float32)
    for b in range(GROUPS):
        feeds = lax.broadcasted_iota(jnp.int32, (NS, FEEDS), 0) + b * NS
        mine = jnp.sum(jnp.where(feeds == feed_ref[...], code, 0.0), axis=1, keepdims=True)
        lanes = lax.broadcasted_iota(jnp.int32, (NS, GROUPS * ROOM), 1)
        first_ref[b] = as_onehot(mine.astype(jnp.int32) == lanes)
    north = order_ref[...] % NS
    wanted = order_ref[...] - north + jnp.where(north <= NS // 2, north, NS + NS // 2 - north)
    pick_ref[...] = as_onehot(column_of(wanted) == lax.broadcasted_iota(jnp.int32, (BEAMS, BEAMS), 1))
    deepest_ref[0] = deepest


def route(slot_feed, beam_order, table):
    whole = pl.BlockSpec(memory_space=pltpu.VMEM)
    return pl.pallas_call(
        route_kernel,
        in_specs=[whole, whole, whole],
        out_specs=[whole, whole, whole, pl.BlockSpec(memory_space=pltpu.SMEM)],
        out_shape=[
            jax.ShapeDtypeStruct((GROUPS, NS, GROUPS * ROOM), jnp.bfloat16),
            jax.ShapeDtypeStruct((GROUPS, GROUPS * ROOM, NS), jnp.bfloat16),
            jax.ShapeDtypeStruct((BEAMS, BEAMS), jnp.bfloat16),
            jax.ShapeDtypeStruct((1,), jnp.int32),
        ],
        compiler_params=pltpu.CompilerParams(vmem_limit_bytes=56 * 2**20),
        name="route",
    )(slot_feed, beam_order, table)


def form_kernel(
    volt_ref, feed_ref, table_ref, first_ref, second_ref, pick_ref, deepest_ref, out_ref, first_tiles, second_tiles, unit_ref
):
    chans = volt_ref.shape[0]
    half = NS // 2
    t = pl.program_id(1)

    @pl.when(t == 0)
    def _():
        unit_ref[...] = jnp.zeros_like(unit_ref)

    edge = lax.broadcasted_iota(jnp.int32, (chans, half), 1) == 0

    def west(tiles_ref, part):
        re, im = [], []
        for y in range(CYL):
            tile = 2 * y + part
            re.append(tiles_ref[tile, pl.ds(0, chans, stride=2), :])
            im.append(tiles_ref[tile, pl.ds(1, chans, stride=2), :])
        a_re, a_im = re[0] + re[2], im[0] + im[2]
        b_re, b_im = re[0] - re[2], im[0] - im[2]
        c_re, c_im = re[1] + re[3], im[1] + im[3]
        d_re, d_im = re[1] - re[3], im[1] - im[3]
        return [
            (a_re + c_re, a_im + c_im),
            (b_re + d_im, b_im - d_re),
            (a_re - c_re, a_im - c_im),
            (b_re - d_im, b_im + d_re),
        ]

    def add_power(power, tiles_ref):
        for e, ((c_re, c_im), (s_re, s_im)) in enumerate(zip(west(tiles_ref, 0), west(tiles_ref, 1))):
            t_re, t_im = jnp.where(edge, 0.0, s_re), jnp.where(edge, 0.0, s_im)
            u_re, u_im = c_re + t_im, c_im - t_re
            v_re, v_im = jnp.where(edge, s_re, c_re - t_im), jnp.where(edge, s_im, c_im + t_re)
            for at, (w_re, w_im) in ((2 * e, (u_re, u_im)), (2 * e + 1, (v_re, v_im))):
                square = w_re * w_re + w_im * w_im
                power[at] = square if power[at] is None else power[at] + square

    def finish(power):
        power = jnp.concatenate(power, axis=1)
        most = jnp.maximum(jnp.max(power, axis=1, keepdims=True), 1e-30)
        level = jnp.ceil(jnp.log2(most) * STEPS) + 1.0
        scale = LEVELS * jnp.exp2(level * (-1.0 / STEPS))
        code = (power * scale + (ROUND - HALF)) - ROUND
        high = ((code * (1.0 / 256.0) - (0.5 - 1.0 / 512.0) + ROUND) - ROUND) * 256.0
        low = (code - high).astype(jnp.bfloat16)
        total = None
        for piece in (high.astype(jnp.bfloat16), low):
            part = lax.dot_general(
                pick_ref[...], piece, (((1,), (1,)), ((), ())), preferred_element_type=jnp.float32
            )
            total = part if total is None else total + part
        total = total.reshape(BEAMS // 8, 8, chans)
        both = jnp.concatenate([total[:, :, : chans // 2], total[:, :, chans // 2 :]], axis=1)
        out_ref[:, pl.ds(pl.multiple_of(16 * t, 16), 16), :] = both.astype(jnp.int32).astype(jnp.int16)
        levels = jnp.transpose(jnp.broadcast_to(level, (chans, 128)))[:1]
        unit_ref[pl.ds(2 * t, 1), :] = levels[:, : chans // 2]
        unit_ref[pl.ds(2 * t + 1, 1), :] = levels[:, chans // 2 :]

    @pl.when(deepest_ref[0] < ROOM)
    def _():
        rows = volt_ref[:, 0].reshape(2 * chans, FEEDS)
        low_half = lax.broadcasted_iota(jnp.int32, (2 * chans, half), 1) < ROOM
        pieces = [[] for _ in range(GROUPS)]
        for q in range(GROUPS // 2):
            ways = []
            for b in (2 * q, 2 * q + 1):
                way = jnp.dot(
                    rows[:, b * NS : (b + 1) * NS], first_ref[b], preferred_element_type=jnp.float32
                )
                ways.append(way)
            for v in range(GROUPS // 2):
                one = ways[0][:, v * half : (v + 1) * half]
                two = ways[1][:, v * half : (v + 1) * half]
                pieces[2 * v].append(jnp.where(low_half, one, two).astype(jnp.bfloat16))
                pieces[2 * v + 1].append(jnp.where(low_half, two, one).astype(jnp.bfloat16))
        power = [None] * (2 * CYL)
        for p, tiles_ref in enumerate((first_tiles, second_tiles)):
            for y in range(CYL):
                d = p * CYL + y
                wave = jnp.dot(
                    jnp.concatenate(pieces[d], axis=1), second_ref[d], preferred_element_type=jnp.float32
                )
                tiles_ref[2 * y] = wave[:, :half]
                tiles_ref[2 * y + 1] = wave[:, half:]
            add_power(power, tiles_ref)
        finish(power)

    @pl.when(deepest_ref[0] >= ROOM)
    def _():
        rows = volt_ref[:, 0].reshape(2 * chans, FEEDS)
        power = [None] * (2 * CYL)
        for d in range(GROUPS):
            tiles_ref, y = (first_tiles, second_tiles)[d // CYL], d % CYL
            feeds = lax.broadcasted_iota(jnp.int32, (FEEDS, NS), 0)
            place = as_onehot(feeds == feed_ref[:, d * NS : (d + 1) * NS])
            slots = jnp.dot(rows, place, preferred_element_type=jnp.float32).astype(jnp.bfloat16)
            wave = jnp.dot(slots, table_ref[...], preferred_element_type=jnp.float32)
            tiles_ref[2 * y] = wave[:, :half]
            tiles_ref[2 * y + 1] = wave[:, half:]
        add_power(power, first_tiles)
        add_power(power, second_tiles)
        finish(power)

    @pl.when(t == pl.num_programs(1) - 1)
    def _():
        levels = jnp.concatenate([unit_ref[...], jnp.zeros_like(unit_ref)], axis=0)
        levels = levels.astype(jnp.int32).astype(jnp.int16)
        groups = out_ref.shape[0]
        out_ref[:, SAMPLE_ROWS:, :] = jnp.broadcast_to(
            levels[None, : out_ref.shape[1] - SAMPLE_ROWS], (groups, out_ref.shape[1] - SAMPLE_ROWS, chans // 2)
        )


def form_beams(voltages, slot_feed, table, first, second, pick, deepest, chunk, chans):
    samples = voltages.shape[1]
    block = 256
    steps = chans // block
    base = chunk * steps
    groups = BEAMS // 8
    whole = pl.BlockSpec(memory_space=pltpu.VMEM)
    return pl.pallas_call(
        form_kernel,
        grid=(steps, samples),
        in_specs=[
            pl.BlockSpec((block, 1, 2, FEEDS), lambda c, t: (base + c, t, 0, 0)),
            whole,
            whole,
            whole,
            whole,
            whole,
            pl.BlockSpec(memory_space=pltpu.SMEM),
        ],
        out_specs=pl.BlockSpec((groups, ROWS, block // 2), lambda c, t: (0, 0, c)),
        out_shape=jax.ShapeDtypeStruct((groups, ROWS, chans // 2), jnp.int16),
        scratch_shapes=[
            pltpu.VMEM((FEEDS // 256, 2 * block, 128), jnp.float32),
            pltpu.VMEM((FEEDS // 256, 2 * block, 128), jnp.float32),
            pltpu.VMEM((8, block // 2), jnp.float32),
        ],
        compiler_params=pltpu.CompilerParams(vmem_limit_bytes=56 * 2**20),
        cost_estimate=pl.CostEstimate(
            flops=int(2 * chans * samples * (2 * FEEDS * 512 + 2 * 8 * 512 * 256 + 2 * BEAMS * BEAMS)),
            bytes_accessed=chans * samples * 2 * FEEDS * 4,
            transcendentals=0,
        ),
        name="form_beams",
    )(voltages, slot_feed, table, first, second, pick, deepest)


def normal_rows(held_ref, at):
    shards = held_ref.shape[0] // TOGETHER
    samples = TIME // shards
    half = held_ref.shape[-1]
    parts = []
    for shard in range(shards):
        block = held_ref.at[at * shards + shard]
        level = block[SAMPLE_ROWS:, :].astype(jnp.float32)
        unit = jnp.exp2(level * (1.0 / STEPS)) * (0.25 / LEVELS)
        for t in range(samples):
            code = block[16 * t : 16 * t + 16, :].astype(jnp.float32) + HALF
            ends = [
                code[8 * h : 8 * h + 8] * unit[2 * t + h : 2 * t + h + 1] for h in range(2)
            ]
            parts.append(jnp.concatenate(ends, axis=1))
    average = functools.reduce(jnp.add, parts) / TIME
    rows = [
        jnp.concatenate([parts[i] - average, parts[i + 1] - average], axis=0).astype(jnp.bfloat16)
        for i in range(0, TIME, 2)
    ]
    return jnp.concatenate(rows, axis=0)


def add_delayed(held_ref, lag_ref, trial_ref, total_ref):
    normals, delays = [], []
    for at in range(TOGETHER):
        normals.append(normal_rows(held_ref, at))
        lag = column_of(lag_ref[at])
        delays.append(jnp.floor(lag * trial_ref[...] * (1.0 / QUANT)).astype(jnp.bfloat16))
    normal = jnp.concatenate(normals, axis=1)
    delay = jnp.concatenate(delays, axis=0)
    one, zero = jnp.ones((), jnp.bfloat16), jnp.zeros((), jnp.bfloat16)
    for k in range(MAXD + 1):
        onehot = jnp.where(delay == jnp.bfloat16(k), one, zero)
        keep = TIME * 8 - 8 * k
        rows = -(-keep // 16) * 16
        part = jnp.dot(normal[:rows], onehot, preferred_element_type=jnp.float32)
        total_ref[8 * k :, :] += part[:keep]


def sum_kernel(held_ref, lag_ref, trial_ref, total_ref):
    @pl.when(pl.program_id(0) == 0)
    def _():
        total_ref[...] = jnp.zeros_like(total_ref)

    add_delayed(held_ref, lag_ref, trial_ref, total_ref)


def share_kernel(
    held_ref, lag_ref, trial_ref, before_ref, out_ref, total_ref, landed_ref, send_sem, recv_sem
):
    shards, rows = landed_ref.shape[0], landed_ref.shape[1]
    step = pl.program_id(0)
    me = lax.axis_index("tm")
    barrier = pltpu.get_barrier_semaphore()

    def device(other):
        return (lax.axis_index("sub"), other)

    def copy(i):
        other = lax.rem(me + i, shards)
        return pltpu.make_async_remote_copy(
            src_ref=total_ref.at[pl.ds(pl.multiple_of(other * rows, 8), rows), :],
            dst_ref=landed_ref.at[me],
            send_sem=send_sem.at[i],
            recv_sem=recv_sem.at[i],
            device_id=device(other),
            device_id_type=pl.DeviceIdType.MESH,
        )

    @pl.when(step == 0)
    def _():
        for i in range(1, shards):
            pl.semaphore_signal(
                barrier, inc=1, device_id=device(lax.rem(me + i, shards)), device_id_type=pl.DeviceIdType.MESH
            )
        total_ref[...] = before_ref[...]

    add_delayed(held_ref, lag_ref, trial_ref, total_ref)

    @pl.when(step == pl.num_programs(0) - 1)
    def _():
        pl.semaphore_wait(barrier, shards - 1)
        copies = [copy(i) for i in range(1, shards)]
        for each in copies:
            each.start()
        landed_ref[me] = total_ref[pl.ds(pl.multiple_of(me * rows, 8), rows), :]
        for each in copies:
            each.wait()
        out_ref[...] = landed_ref[...]


def sum_delays(held, lags, trials, before):
    chans = 2 * held.shape[-1]
    subs = lags.shape[0]
    shards = held.shape[0] // subs
    rows = TIME * 8
    whole = pl.BlockSpec(memory_space=pltpu.VMEM)
    in_specs = [
        pl.BlockSpec((TOGETHER * shards, ROWS, chans // 2), lambda s: (s, 0, 0)),
        pl.BlockSpec((TOGETHER, 1, chans), lambda s: (s, 0, 0)),
        whole,
    ]
    cost = pl.CostEstimate(
        flops=2 * subs * chans * rows * NDM * 7,
        bytes_accessed=subs * chans * rows * 2,
        transcendentals=0,
    )
    if before is None:
        return pl.pallas_call(
            sum_kernel,
            grid=(subs // TOGETHER,),
            in_specs=in_specs,
            out_specs=pl.BlockSpec((rows, NDM), lambda s: (0, 0)),
            out_shape=jax.ShapeDtypeStruct((rows, NDM), jnp.float32),
            compiler_params=pltpu.CompilerParams(vmem_limit_bytes=56 * 2**20),
            cost_estimate=cost,
            name="sum_delays",
        )(held, lags, trials)
    return pl.pallas_call(
        share_kernel,
        grid=(subs // TOGETHER,),
        in_specs=in_specs + [whole],
        out_specs=pl.BlockSpec((shards, rows // shards, NDM), lambda s: (0, 0, 0)),
        out_shape=jax.ShapeDtypeStruct((shards, rows // shards, NDM), jnp.float32),
        scratch_shapes=[
            pltpu.VMEM((rows, NDM), jnp.float32),
            pltpu.VMEM((shards, rows // shards, NDM), jnp.float32),
            pltpu.SemaphoreType.DMA((shards,)),
            pltpu.SemaphoreType.DMA((shards,)),
        ],
        compiler_params=pltpu.CompilerParams(
            vmem_limit_bytes=56 * 2**20, collective_id=0, has_side_effects=True
        ),
        cost_estimate=cost,
        name="sum_and_share",
    )(held, lags, trials, before)


def per_device(voltages, slot_feed, chan_lag, trial_dm, beam_order):
    subs = lax.axis_size("sub")
    table = jnp.asarray(half_table())
    lags = chan_lag.astype(jnp.float32).reshape(subs, CHUNKS, -1)
    trials = trial_dm.astype(jnp.float32).reshape(1, NDM)
    feeds = slot_feed.reshape(1, FEEDS)
    order = beam_order.reshape(1, BEAMS)
    chans = voltages.shape[0] // CHUNKS
    total = None
    first, second, pick, deepest = route(feeds, order, table)
    for chunk in range(CHUNKS):
        formed = form_beams(voltages, feeds, table, first, second, pick, deepest, chunk, chans)
        held = lax.all_to_all(formed, AXES, 0, 0)
        total = sum_delays(held, lags[:, chunk : chunk + 1], trials, total)
    shards, samples = total.shape[0], voltages.shape[1]
    parts = total.reshape(shards, samples, 8, NDM).transpose(0, 2, 1, 3)
    return parts.reshape(shards * 8, samples, NDM) * (1.0 / math.sqrt(CHANNELS))


def solution(mesh):
    placed = (P("sub", "tm", None, None), P(), P(), P(), P())
    return jax.shard_map(
        per_device, mesh=mesh, in_specs=placed, out_specs=P("sub", "tm", None), check_vma=False
    )
```

```python
import functools
import math

import jax
import jax.numpy as jnp
import ml_dtypes
import numpy as np
from jax import lax
from jax.experimental import pallas as pl
from jax.experimental.pallas import tpu as pltpu
from jax.sharding import PartitionSpec as P

NS = 256
CYL = 4
POL = 2
CHANNELS = 8192
NDM = 512
MAXD = 6
QUANT = 2796202
FEEDS = 2048
BEAMS = 1024
TIME = 24
CHUNKS = 2
LEVELS = 65535.0
HALF = 32768.0
STEPS = 256.0
ROUND = 12582912.0
TOGETHER = 8
GROUPS = 8
ROOM = 64
SAMPLE_ROWS = 48
ROWS = 56
AXES = ("sub", "tm")


def half_table():
    n = np.arange(NS)[:, None]
    m = np.arange(NS // 2)[None, :]
    angles = (n * m % NS) * (2.0 * math.pi / NS)
    cosine = np.cos(angles) / math.sqrt(NS)
    sine = np.sin(angles) / math.sqrt(NS)
    sine[:, 0] = np.cos((np.arange(NS) * (NS // 2) % NS) * (2.0 * math.pi / NS)) / math.sqrt(NS)
    return np.concatenate([cosine, sine], axis=1).astype(np.float32).astype(ml_dtypes.bfloat16)


def as_onehot(hit):
    return hit.astype(jnp.float32).astype(jnp.bfloat16)


def column_of(row):
    return jnp.transpose(jnp.broadcast_to(row, (8, row.shape[1])))[:, :1]


def route_kernel(feed_ref, order_ref, table_ref, first_ref, second_ref, pick_ref, deepest_ref):
    deepest = jnp.zeros((), jnp.int32)
    codes = []
    above = lax.broadcasted_iota(jnp.int32, (NS, NS), 0) < lax.broadcasted_iota(jnp.int32, (NS, NS), 1)
    for d in range(GROUPS):
        block = feed_ref[:, d * NS : (d + 1) * NS] // NS
        same = (column_of(block) == block) & above
        rank = jnp.sum(same.astype(jnp.float32), axis=0, keepdims=True).astype(jnp.int32)
        deepest = jnp.maximum(deepest, jnp.max(rank))
        odd = block % 2
        flip = odd if d % 2 == 0 else 1 - odd
        codes.append((jnp.where(odd == 0, d, d ^ 1)) * ROOM + rank)
        place = block // 2 * (2 * ROOM) + flip * ROOM + rank
        hit = lax.broadcasted_iota(jnp.int32, (GROUPS * ROOM, NS), 0) == place
        second_ref[d] = jnp.dot(
            as_onehot(hit), table_ref[...], preferred_element_type=jnp.float32
        ).astype(jnp.bfloat16)
    code = jnp.concatenate(codes, axis=1)
    within = as_onehot(lax.broadcasted_iota(jnp.int32, (NS, FEEDS), 0) == feed_ref[...] % NS)
    mine = lax.broadcasted_iota(jnp.int32, (GROUPS, FEEDS), 0) == feed_ref[...] // NS
    digits = [jnp.where(mine, digit, 0).astype(jnp.float32) for digit in (code // 16 * 16, code % 16)]
    columns = lax.dot_general(
        within,
        jnp.concatenate(digits, axis=0).astype(jnp.bfloat16),
        (((1,), (1,)), ((), ())),
        preferred_element_type=jnp.float32,
    ).astype(jnp.int32)
    lanes = lax.broadcasted_iota(jnp.int32, (NS, GROUPS * ROOM), 1)
    for b in range(GROUPS):
        column = columns[:, b : b + 1] + columns[:, GROUPS + b : GROUPS + b + 1]
        first_ref[b] = as_onehot(column == lanes)
    north = order_ref[...] % NS
    wanted = order_ref[...] - north + jnp.where(north <= NS // 2, north, NS + NS // 2 - north)
    pick_ref[...] = as_onehot(column_of(wanted) == lax.broadcasted_iota(jnp.int32, (BEAMS, BEAMS), 1))
    deepest_ref[0] = deepest


def route(slot_feed, beam_order, table):
    whole = pl.BlockSpec(memory_space=pltpu.VMEM)
    return pl.pallas_call(
        route_kernel,
        in_specs=[whole, whole, whole],
        out_specs=[whole, whole, whole, pl.BlockSpec(memory_space=pltpu.SMEM)],
        out_shape=[
            jax.ShapeDtypeStruct((GROUPS, NS, GROUPS * ROOM), jnp.bfloat16),
            jax.ShapeDtypeStruct((GROUPS, GROUPS * ROOM, NS), jnp.bfloat16),
            jax.ShapeDtypeStruct((BEAMS, BEAMS), jnp.bfloat16),
            jax.ShapeDtypeStruct((1,), jnp.int32),
        ],
        compiler_params=pltpu.CompilerParams(vmem_limit_bytes=56 * 2**20),
        name="route",
    )(slot_feed, beam_order, table)


def form_kernel(
    volt_ref, feed_ref, table_ref, first_ref, second_ref, pick_ref, deepest_ref, out_ref, first_tiles, second_tiles, unit_ref
):
    chans = volt_ref.shape[0]
    half = NS // 2
    t = pl.program_id(1)

    @pl.when(t == 0)
    def _():
        unit_ref[...] = jnp.zeros_like(unit_ref)

    edge = lax.broadcasted_iota(jnp.int32, (chans, half), 1) == 0

    def west(tiles_ref, part):
        re, im = [], []
        for y in range(CYL):
            tile = 2 * y + part
            re.append(tiles_ref[tile, pl.ds(0, chans, stride=2), :])
            im.append(tiles_ref[tile, pl.ds(1, chans, stride=2), :])
        a_re, a_im = re[0] + re[2], im[0] + im[2]
        b_re, b_im = re[0] - re[2], im[0] - im[2]
        c_re, c_im = re[1] + re[3], im[1] + im[3]
        d_re, d_im = re[1] - re[3], im[1] - im[3]
        return [
            (a_re + c_re, a_im + c_im),
            (b_re + d_im, b_im - d_re),
            (a_re - c_re, a_im - c_im),
            (b_re - d_im, b_im + d_re),
        ]

    def add_power(power, tiles_ref):
        for e, ((c_re, c_im), (s_re, s_im)) in enumerate(zip(west(tiles_ref, 0), west(tiles_ref, 1))):
            t_re, t_im = jnp.where(edge, 0.0, s_re), jnp.where(edge, 0.0, s_im)
            u_re, u_im = c_re + t_im, c_im - t_re
            v_re, v_im = jnp.where(edge, s_re, c_re - t_im), jnp.where(edge, s_im, c_im + t_re)
            for at, (w_re, w_im) in ((2 * e, (u_re, u_im)), (2 * e + 1, (v_re, v_im))):
                square = w_re * w_re + w_im * w_im
                power[at] = square if power[at] is None else power[at] + square

    def finish(power):
        power = jnp.concatenate(power, axis=1)
        most = jnp.maximum(jnp.max(power, axis=1, keepdims=True), 1e-30)
        level = jnp.ceil(jnp.log2(most) * STEPS) + 1.0
        scale = LEVELS * jnp.exp2(level * (-1.0 / STEPS))
        code = (power * scale + (ROUND - HALF)) - ROUND
        high = ((code * (1.0 / 256.0) - (0.5 - 1.0 / 512.0) + ROUND) - ROUND) * 256.0
        low = (code - high).astype(jnp.bfloat16)
        total = None
        for piece in (high.astype(jnp.bfloat16), low):
            part = lax.dot_general(
                pick_ref[...], piece, (((1,), (1,)), ((), ())), preferred_element_type=jnp.float32
            )
            total = part if total is None else total + part
        total = total.reshape(BEAMS // 8, 8, chans)
        both = jnp.concatenate([total[:, :, : chans // 2], total[:, :, chans // 2 :]], axis=1)
        out_ref[:, pl.ds(pl.multiple_of(16 * t, 16), 16), :] = both.astype(jnp.int32).astype(jnp.int16)
        levels = jnp.transpose(jnp.broadcast_to(level, (chans, 128)))[:1]
        unit_ref[pl.ds(2 * t, 1), :] = levels[:, : chans // 2]
        unit_ref[pl.ds(2 * t + 1, 1), :] = levels[:, chans // 2 :]

    @pl.when(deepest_ref[0] < ROOM)
    def _():
        rows = volt_ref[:, 0].reshape(2 * chans, FEEDS)
        low_half = lax.broadcasted_iota(jnp.int32, (2 * chans, half), 1) < ROOM
        pieces = [[] for _ in range(GROUPS)]
        for q in range(GROUPS // 2):
            ways = []
            for b in (2 * q, 2 * q + 1):
                way = jnp.dot(
                    rows[:, b * NS : (b + 1) * NS], first_ref[b], preferred_element_type=jnp.float32
                )
                ways.append(way)
            for v in range(GROUPS // 2):
                one = ways[0][:, v * half : (v + 1) * half]
                two = ways[1][:, v * half : (v + 1) * half]
                pieces[2 * v].append(jnp.where(low_half, one, two).astype(jnp.bfloat16))
                pieces[2 * v + 1].append(jnp.where(low_half, two, one).astype(jnp.bfloat16))
        power = [None] * (2 * CYL)
        for p, tiles_ref in enumerate((first_tiles, second_tiles)):
            for y in range(CYL):
                d = p * CYL + y
                wave = jnp.dot(
                    jnp.concatenate(pieces[d], axis=1), second_ref[d], preferred_element_type=jnp.float32
                )
                tiles_ref[2 * y] = wave[:, :half]
                tiles_ref[2 * y + 1] = wave[:, half:]
            add_power(power, tiles_ref)
        finish(power)

    @pl.when(deepest_ref[0] >= ROOM)
    def _():
        rows = volt_ref[:, 0].reshape(2 * chans, FEEDS)
        power = [None] * (2 * CYL)
        for d in range(GROUPS):
            tiles_ref, y = (first_tiles, second_tiles)[d // CYL], d % CYL
            feeds = lax.broadcasted_iota(jnp.int32, (FEEDS, NS), 0)
            place = as_onehot(feeds == feed_ref[:, d * NS : (d + 1) * NS])
            slots = jnp.dot(rows, place, preferred_element_type=jnp.float32).astype(jnp.bfloat16)
            wave = jnp.dot(slots, table_ref[...], preferred_element_type=jnp.float32)
            tiles_ref[2 * y] = wave[:, :half]
            tiles_ref[2 * y + 1] = wave[:, half:]
        add_power(power, first_tiles)
        add_power(power, second_tiles)
        finish(power)

    @pl.when(t == pl.num_programs(1) - 1)
    def _():
        levels = jnp.concatenate([unit_ref[...], jnp.zeros_like(unit_ref)], axis=0)
        levels = levels.astype(jnp.int32).astype(jnp.int16)
        groups = out_ref.shape[0]
        out_ref[:, SAMPLE_ROWS:, :] = jnp.broadcast_to(
            levels[None, : out_ref.shape[1] - SAMPLE_ROWS], (groups, out_ref.shape[1] - SAMPLE_ROWS, chans // 2)
        )


def form_beams(voltages, slot_feed, table, first, second, pick, deepest, chunk, chans):
    samples = voltages.shape[1]
    block = 256
    steps = chans // block
    base = chunk * steps
    groups = BEAMS // 8
    whole = pl.BlockSpec(memory_space=pltpu.VMEM)
    return pl.pallas_call(
        form_kernel,
        grid=(steps, samples),
        in_specs=[
            pl.BlockSpec((block, 1, 2, FEEDS), lambda c, t: (base + c, t, 0, 0)),
            whole,
            whole,
            whole,
            whole,
            whole,
            pl.BlockSpec(memory_space=pltpu.SMEM),
        ],
        out_specs=pl.BlockSpec((groups, ROWS, block // 2), lambda c, t: (0, 0, c)),
        out_shape=jax.ShapeDtypeStruct((groups, ROWS, chans // 2), jnp.int16),
        scratch_shapes=[
            pltpu.VMEM((FEEDS // 256, 2 * block, 128), jnp.float32),
            pltpu.VMEM((FEEDS // 256, 2 * block, 128), jnp.float32),
            pltpu.VMEM((8, block // 2), jnp.float32),
        ],
        compiler_params=pltpu.CompilerParams(vmem_limit_bytes=56 * 2**20),
        cost_estimate=pl.CostEstimate(
            flops=int(2 * chans * samples * (2 * FEEDS * 512 + 2 * 8 * 512 * 256 + 2 * BEAMS * BEAMS)),
            bytes_accessed=chans * samples * 2 * FEEDS * 4,
            transcendentals=0,
        ),
        name="form_beams",
    )(voltages, slot_feed, table, first, second, pick, deepest)


def normal_rows(held_ref, at):
    shards = held_ref.shape[0] // TOGETHER
    samples = TIME // shards
    half = held_ref.shape[-1]
    parts = []
    for shard in range(shards):
        block = held_ref.at[at * shards + shard]
        level = block[SAMPLE_ROWS:, :].astype(jnp.float32)
        unit = jnp.exp2(level * (1.0 / STEPS)) * (0.25 / LEVELS)
        for t in range(samples):
            code = block[16 * t : 16 * t + 16, :].astype(jnp.float32) + HALF
            ends = [
                code[8 * h : 8 * h + 8] * unit[2 * t + h : 2 * t + h + 1] for h in range(2)
            ]
            parts.append(jnp.concatenate(ends, axis=1))
    average = functools.reduce(jnp.add, parts) / TIME
    rows = [
        jnp.concatenate([parts[i] - average, parts[i + 1] - average], axis=0).astype(jnp.bfloat16)
        for i in range(0, TIME, 2)
    ]
    return jnp.concatenate(rows, axis=0)


def add_delayed(held_ref, lag_ref, trial_ref, total_ref):
    normals, delays = [], []
    for at in range(TOGETHER):
        normals.append(normal_rows(held_ref, at))
        lag = column_of(lag_ref[at])
        delays.append(jnp.floor(lag * trial_ref[...] * (1.0 / QUANT)).astype(jnp.bfloat16))
    normal = jnp.concatenate(normals, axis=1)
    delay = jnp.concatenate(delays, axis=0)
    one, zero = jnp.ones((), jnp.bfloat16), jnp.zeros((), jnp.bfloat16)
    for k in range(MAXD + 1):
        onehot = jnp.where(delay == jnp.bfloat16(k), one, zero)
        keep = TIME * 8 - 8 * k
        rows = -(-keep // 16) * 16
        part = jnp.dot(normal[:rows], onehot, preferred_element_type=jnp.float32)
        total_ref[8 * k :, :] += part[:keep]


def sum_kernel(held_ref, lag_ref, trial_ref, total_ref):
    @pl.when(pl.program_id(0) == 0)
    def _():
        total_ref[...] = jnp.zeros_like(total_ref)

    add_delayed(held_ref, lag_ref, trial_ref, total_ref)


def share_kernel(
    held_ref, lag_ref, trial_ref, before_ref, out_ref, total_ref, landed_ref, send_sem, recv_sem
):
    shards, rows = landed_ref.shape[0], landed_ref.shape[1]
    step = pl.program_id(0)
    me = lax.axis_index("tm")
    barrier = pltpu.get_barrier_semaphore()

    def device(other):
        return (lax.axis_index("sub"), other)

    def copy(i):
        other = lax.rem(me + i, shards)
        return pltpu.make_async_remote_copy(
            src_ref=total_ref.at[pl.ds(pl.multiple_of(other * rows, 8), rows), :],
            dst_ref=landed_ref.at[me],
            send_sem=send_sem.at[i],
            recv_sem=recv_sem.at[i],
            device_id=device(other),
            device_id_type=pl.DeviceIdType.MESH,
        )

    @pl.when(step == 0)
    def _():
        for i in range(1, shards):
            pl.semaphore_signal(
                barrier, inc=1, device_id=device(lax.rem(me + i, shards)), device_id_type=pl.DeviceIdType.MESH
            )
        total_ref[...] = before_ref[...]

    add_delayed(held_ref, lag_ref, trial_ref, total_ref)

    @pl.when(step == pl.num_programs(0) - 1)
    def _():
        pl.semaphore_wait(barrier, shards - 1)
        copies = [copy(i) for i in range(1, shards)]
        for each in copies:
            each.start()
        landed_ref[me] = total_ref[pl.ds(pl.multiple_of(me * rows, 8), rows), :]
        for each in copies:
            each.wait()
        out_ref[...] = landed_ref[...]


def sum_delays(held, lags, trials, before):
    chans = 2 * held.shape[-1]
    subs = lags.shape[0]
    shards = held.shape[0] // subs
    rows = TIME * 8
    whole = pl.BlockSpec(memory_space=pltpu.VMEM)
    in_specs = [
        pl.BlockSpec((TOGETHER * shards, ROWS, chans // 2), lambda s: (s, 0, 0)),
        pl.BlockSpec((TOGETHER, 1, chans), lambda s: (s, 0, 0)),
        whole,
    ]
    cost = pl.CostEstimate(
        flops=2 * subs * chans * rows * NDM * 7,
        bytes_accessed=subs * chans * rows * 2,
        transcendentals=0,
    )
    if before is None:
        return pl.pallas_call(
            sum_kernel,
            grid=(subs // TOGETHER,),
            in_specs=in_specs,
            out_specs=pl.BlockSpec((rows, NDM), lambda s: (0, 0)),
            out_shape=jax.ShapeDtypeStruct((rows, NDM), jnp.float32),
            compiler_params=pltpu.CompilerParams(vmem_limit_bytes=56 * 2**20),
            cost_estimate=cost,
            name="sum_delays",
        )(held, lags, trials)
    return pl.pallas_call(
        share_kernel,
        grid=(subs // TOGETHER,),
        in_specs=in_specs + [whole],
        out_specs=pl.BlockSpec((shards, rows // shards, NDM), lambda s: (0, 0, 0)),
        out_shape=jax.ShapeDtypeStruct((shards, rows // shards, NDM), jnp.float32),
        scratch_shapes=[
            pltpu.VMEM((rows, NDM), jnp.float32),
            pltpu.VMEM((shards, rows // shards, NDM), jnp.float32),
            pltpu.SemaphoreType.DMA((shards,)),
            pltpu.SemaphoreType.DMA((shards,)),
        ],
        compiler_params=pltpu.CompilerParams(
            vmem_limit_bytes=56 * 2**20, collective_id=0, has_side_effects=True
        ),
        cost_estimate=cost,
        name="sum_and_share",
    )(held, lags, trials, before)


def per_device(voltages, slot_feed, chan_lag, trial_dm, beam_order):
    subs = lax.axis_size("sub")
    table = jnp.asarray(half_table())
    lags = chan_lag.astype(jnp.float32).reshape(subs, CHUNKS, -1)
    trials = trial_dm.astype(jnp.float32).reshape(1, NDM)
    feeds = slot_feed.reshape(1, FEEDS)
    order = beam_order.reshape(1, BEAMS)
    chans = voltages.shape[0] // CHUNKS
    total = None
    first, second, pick, deepest = route(feeds, order, table)
    for chunk in range(CHUNKS):
        formed = form_beams(voltages, feeds, table, first, second, pick, deepest, chunk, chans)
        held = lax.all_to_all(formed, AXES, 0, 0)
        total = sum_delays(held, lags[:, chunk : chunk + 1], trials, total)
    shards, samples = total.shape[0], voltages.shape[1]
    parts = total.reshape(shards, samples, 8, NDM).transpose(0, 2, 1, 3)
    return parts.reshape(shards * 8, samples, NDM) * (1.0 / math.sqrt(CHANNELS))


def solution(mesh):
    placed = (P("sub", "tm", None, None), P(), P(), P(), P())
    return jax.shard_map(
        per_device, mesh=mesh, in_specs=placed, out_specs=P("sub", "tm", None), check_vma=False
    )
```
